128 devices in a mesh: member: 4 (over x), slab: 32 (over z, y, core).
Axes of the slice: x: 4, y: 4, z: 4, core: 2. Of those that a mesh axis runs over, the one named last changes fastest.
Arguments:
- ensemble: float32 [80, 1572864], P('member', 'slab'), may hold values from -6 to 6
- block_order: int32 [4], replicated, may hold values from 0 to 3, each once
- obs_owner: int32 [4, 256], replicated, may hold values from 0 to 127
- interp_cells: int32 [4, 256, 4], replicated, may hold values from 0 to 12287
- interp_weight: float32 [4, 256, 4], replicated, may hold values from 0.1 to 0.5
- obs_radius: int32 [4, 256], replicated, may hold values from 12288 to 49151
- obs_value: float32 [4, 256], replicated, may hold values from -6 to 6
- obs_variance: float32 [4, 256], replicated, may hold values from 0.25 to 2
Outputs:
- posterior: float32 [80, 1572864], P('member', 'slab')
The draws below stay inside these ranges and needn't reach their ends.
Inputs may be any that keep to these rules, and one draw needn't show every extreme that they name: `block_order`: a permutation of the block numbers. `obs_owner`: the index of the block of 12288 consecutive state cells that holds the observation.
All inputs are finite; a program needn't handle non-finite values.
Results may differ from the reference program's by a relative error of at most 0.0001.
Values sent between devices are 32-bit elements; how exact they have to be, the bound alone decides.
No kernel may reach another device: no remote copies, remote signals or barrier semaphores. Data moves between devices by JAX's collectives and lax.ppermute only.
A program may use at most 128 MiB of HBM per device.

```python
import math
import jax
import jax.numpy as jnp
import numpy as np
from jax import lax

MEMBERS = 80
CELLS_DEV = 12288
OBS_BLOCK = 256
BLOCKS = 4
POINTS = 4
STATE_CELLS = 1572864
DEVICES = 128


def plant(result, stream_key, low, top_value):
    extent = result.shape
    place = [jax.random.randint(jax.random.fold_in(stream_key, axis), (), 0, extent[axis]) for axis in range(len(extent))]
    result = result.at[tuple(place)].set(low)
    longest = extent.index(max(extent))
    place[longest] = (place[longest] + 1) % extent[longest]
    return result.at[tuple(place)].set(top_value)


def steps_of(stream_key, extent, pieces, least, largest):
    level = 1.0
    for axis_at, blocks in pieces:
        draws = jax.random.uniform(jax.random.fold_in(jax.random.fold_in(stream_key, 6), axis_at), (blocks,), jnp.float32, least / len(pieces), largest / len(pieces))
        level = level * jnp.repeat(jnp.exp(draws), extent[axis_at] // blocks).reshape((-1,) + (1,) * (len(extent) - 1 - axis_at))
    return level


def cumulative_ranks(count, lean):
    portions = [(1 << 20) // math.isqrt(rank ** lean) + 1 for rank in range(1, count + 1)]
    scale = 1 + sum(portions) // (1 << 30)
    return np.cumsum(np.array([max(1, weight // scale) for weight in portions]))


def ranked(key, shape, count, lean):
    table = cumulative_ranks(count, lean)
    ticket = jax.random.randint(jax.random.fold_in(key, 1), shape, 0, int(table[count - 1]))
    grade = jnp.searchsorted(jnp.asarray(table, jnp.int32), ticket, side="right")
    return jax.random.permutation(jax.random.fold_in(key, 2), count)[grade].astype(jnp.int32)


def gaussian(stream_key, extent, scale, bound, shards=(), held_as=jnp.bfloat16):
    values = jax.random.normal(stream_key, extent, jnp.float32) * scale
    if len(shards) > 0:
        values = steps_of(stream_key, extent, shards, -0.22, 0.18) * values
    return jnp.clip(values, min=-bound, max=bound).astype(held_as)


def setup_inputs(seed: int = 0) -> dict:
    key_of = jax.random.split(jax.random.key(seed), 9)
    ensemble = gaussian(key_of[0], (MEMBERS, STATE_CELLS), 1.0, 6.0, ((0, 4), (1, 32)), jnp.float32)
    block_order = jax.random.permutation(key_of[1], BLOCKS).astype(jnp.int32)
    obs_owner = plant(ranked(key_of[2], (BLOCKS, OBS_BLOCK), DEVICES, 2), jax.random.fold_in(key_of[2], 3), 0, DEVICES - 1).astype(jnp.int32)
    interp_cells = plant(jax.random.randint(key_of[3], (BLOCKS, OBS_BLOCK, POINTS), 0, CELLS_DEV), jax.random.fold_in(key_of[3], 1), 0, CELLS_DEV - 1).astype(jnp.int32)
    interp_weight = jnp.clip(jax.random.uniform(key_of[4], (BLOCKS, OBS_BLOCK, POINTS), jnp.float32, 0.1, 0.5), 0.1, 0.5)
    obs_radius = plant(jax.random.randint(key_of[5], (BLOCKS, OBS_BLOCK), CELLS_DEV, 4 * CELLS_DEV), jax.random.fold_in(key_of[5], 1), CELLS_DEV, (4 * CELLS_DEV) - 1).astype(jnp.int32)
    obs_value = gaussian(key_of[6], (BLOCKS, OBS_BLOCK), 1.0, 6.0, (), jnp.float32)
    obs_variance = jnp.clip(jnp.exp(jax.random.uniform(key_of[7], (BLOCKS, OBS_BLOCK), jnp.float32, math.log(0.25), math.log(2.0))), 0.25, 2.0)
    return dict(ensemble=ensemble, block_order=block_order, obs_owner=obs_owner, interp_cells=interp_cells, interp_weight=interp_weight, obs_radius=obs_radius, obs_value=obs_value, obs_variance=obs_variance)


def obs_terms(prior, values, variance):
    ybar = lax.optimization_barrier(jnp.mean(prior, axis=1))
    anomaly_y = prior - ybar[:, None]
    spread = lax.optimization_barrier(jnp.sum(anomaly_y * anomaly_y, axis=1)) / (MEMBERS - 1)
    gain = 1.0 / (spread + variance)
    shrink = -gain / (1.0 + jnp.sqrt(variance * gain))
    coeff = gain * (values - ybar)
    driver = coeff[:, None] + shrink[:, None] * anomaly_y
    return (anomaly_y, driver)

def increment(span, first, anomaly_y, driver, centre, radius):
    anomaly_x = span - lax.optimization_barrier(jnp.mean(span, axis=0))[None, :]
    cov = jnp.einsum('ec,be->cb', anomaly_x, anomaly_y, precision=lax.Precision.HIGHEST) / (MEMBERS - 1)
    positions = first + jnp.arange(span.shape[1], dtype=jnp.int32)
    dist = jnp.abs(positions[:, None] - centre[None, :]).astype(jnp.float32)
    loc = jnp.maximum(jnp.float32(0.0), 1.0 - dist / radius[None, :])
    return span + jnp.einsum('cb,be->ec', loc * cov, driver, precision=lax.Precision.HIGHEST)

def reference(ensemble, block_order, obs_owner, interp_cells, interp_weight, obs_radius, obs_value, obs_variance):
    state = ensemble
    nchunks = STATE_CELLS // CELLS_DEV
    for step in range(BLOCKS):
        which = block_order[step]
        owner = obs_owner[which]
        cells = interp_cells[which]
        weight = interp_weight[which]
        global_cells = (owner[:, None] * CELLS_DEV + cells).astype(jnp.int32)
        picked = state[:, global_cells]
        prior = lax.optimization_barrier(jnp.sum(picked * weight[None], axis=-1)).T
        anomaly_y, driver = obs_terms(prior, obs_value[which], obs_variance[which])
        centre = (owner * CELLS_DEV + cells[:, 0]).astype(jnp.int32)
        radius = obs_radius[which].astype(jnp.float32)
        spans = state.reshape(MEMBERS, nchunks, CELLS_DEV).transpose(1, 0, 2)

        def update(pair):
            span, number = pair
            return increment(span, number * CELLS_DEV, anomaly_y, driver, centre, radius)
        updated = lax.map(update, (spans, jnp.arange(nchunks, dtype=jnp.int32)))
        state = updated.transpose(1, 0, 2).reshape(MEMBERS, STATE_CELLS)
    return state
```

```python
import functools

import jax
import jax.numpy as jnp
from jax import lax
from jax.experimental import pallas as pl
from jax.experimental.pallas import tpu as pltpu
from jax.sharding import PartitionSpec as P

MEMBERS = 80
BLOCKS = 4
POINTS = 4
OBS = 256
GROUPS = 4
ROWS = MEMBERS // GROUPS
CELLS = 12288
CHUNKS = 4
CHUNK = CELLS // CHUNKS
HALF = CHUNK // 2
PACKED = 5 * HALF
TILE = 256
COLS = OBS + (BLOCKS - 1) * POINTS * OBS
PART = COLS // 2
VMEM = 60 * 1024 * 1024

f32 = jnp.float32
bf16 = jnp.bfloat16


def split(x):
    hi = x.astype(bf16)
    lo = (x - hi.astype(f32)).astype(bf16)
    return hi, lo


def whole(n):
    return [pl.BlockSpec(memory_space=pltpu.VMEM)] * n


def params(**kw):
    return pltpu.CompilerParams(vmem_limit_bytes=VMEM, **kw)


def pack_kernel(rank_ref, ens_ref, *outs):
    rank = rank_ref[0]
    for d in range(GROUPS):
        quarter = lax.rem(rank + d, GROUPS)
        for c in range(CHUNKS):
            out = outs[d * CHUNKS + c]
            at = pl.multiple_of(quarter * CELLS + c * CHUNK, 128)
            mid = pl.multiple_of(quarter * CELLS + c * CHUNK + HALF, 128)
            out[:, 0:CHUNK] = ens_ref[0:8, pl.ds(at, CHUNK)]
            out[:, CHUNK : 2 * CHUNK] = ens_ref[8:16, pl.ds(at, CHUNK)]
            out[0:4, 2 * CHUNK : PACKED] = ens_ref[16:20, pl.ds(at, HALF)]
            out[4:8, 2 * CHUNK : PACKED] = ens_ref[16:20, pl.ds(mid, HALF)]


def pack(rank, ensemble):
    return pl.pallas_call(
        pack_kernel,
        out_shape=[jax.ShapeDtypeStruct((8, PACKED), f32)] * (GROUPS * CHUNKS),
        in_specs=[pl.BlockSpec(memory_space=pltpu.SMEM)] + whole(1),
        out_specs=whole(GROUPS * CHUNKS),
        compiler_params=params(),
        cost_estimate=pl.CostEstimate(flops=0, bytes_accessed=8 * 2**20, transcendentals=0),
        name="pack",
    )(rank, ensemble)


def pick_kernel(place_ref, part_ref, weight_ref, ens_ref, keep_ref, send_ref, first, picked):
    lanes = lax.broadcasted_iota(jnp.int32, (8, 128), 1)
    lanes4 = lax.broadcasted_iota(jnp.int32, (4, 128), 1)
    unroll = 16

    def group(g, dst, at):
        def some(s, acc):
            a, b, c = acc
            for u in range(unroll):
                n = s * unroll + u
                place = place_ref[g * 128 + n]
                held = place >= 0
                base = pl.multiple_of((jnp.maximum(place, 0) >> 7) * 128, 128)
                shift = (n - place) & 127
                lane = jnp.where(held, n, -1)
                ta = pltpu.roll(ens_ref[0:8, pl.ds(base, 128)], shift, 1)
                tb = pltpu.roll(ens_ref[8:16, pl.ds(base, 128)], shift, 1)
                tc = pltpu.roll(ens_ref[16:20, pl.ds(base, 128)], shift, 1)
                hit = lanes == lane
                a = jnp.where(hit, ta, a)
                b = jnp.where(hit, tb, b)
                c = jnp.where(lanes4 == lane, tc, c)
            return a, b, c

        zero = jnp.zeros((8, 128), f32)
        a, b, c = lax.fori_loop(0, 128 // unroll, some, (zero, zero, jnp.zeros((4, 128), f32)))
        dst[0:8, pl.ds(at, 128)] = a
        dst[8:16, pl.ds(at, 128)] = b
        dst[16:20, pl.ds(at, 128)] = c

    n_first = POINTS * OBS // 128
    n_later = (BLOCKS - 1) * n_first

    def do_first(g, carry):
        group(g, first, pl.multiple_of(g * 128, 128))
        return carry

    def do_later(g, carry):
        group(g + n_first, picked, pl.multiple_of(OBS + g * 128, 128))
        return carry

    lax.fori_loop(0, n_first, do_first, 0)
    total = first[:, 0:OBS] * weight_ref[0:1, :]
    for k in range(1, POINTS):
        total = total + first[:, k * OBS : (k + 1) * OBS] * weight_ref[k : k + 1, :]
    picked[:, 0:OBS] = total
    lax.fori_loop(0, n_later, do_later, 0)
    part = part_ref[0]
    keep_ref[...] = picked[:, pl.ds(pl.multiple_of(part * PART, 128), PART)]
    send_ref[...] = picked[:, pl.ds(pl.multiple_of((1 - part) * PART, 128), PART)]


def pick(place, part, weight, ensemble):
    smem = pl.BlockSpec(memory_space=pltpu.SMEM)
    return pl.pallas_call(
        pick_kernel,
        out_shape=[jax.ShapeDtypeStruct((ROWS, PART), f32)] * 2,
        in_specs=[smem, smem] + whole(2),
        out_specs=whole(2),
        scratch_shapes=[pltpu.VMEM((ROWS, POINTS * OBS), f32), pltpu.VMEM((ROWS, COLS), f32)],
        compiler_params=params(),
        cost_estimate=pl.CostEstimate(flops=0, bytes_accessed=40 * 2**20, transcendentals=0),
        name="pick",
    )(place, part, weight, ensemble)


def updated(x, place, lhs, driver, centre, inverse):
    n = x.shape[1]
    reps = n // 128
    mean = jnp.sum(x, axis=0, keepdims=True) * f32(1.0 / MEMBERS)
    hi, lo = split(x - mean)
    cov = jnp.dot(lhs, jnp.concatenate([hi, lo, hi], axis=0), preferred_element_type=f32)
    centre = jnp.concatenate([centre] * reps, axis=1)
    inverse = jnp.concatenate([inverse] * reps, axis=1)
    loc = jnp.maximum(f32(0.0), f32(1.0) - jnp.abs(place - centre) * inverse)
    hi, lo = split(loc * cov)
    both = jnp.dot(driver, hi, preferred_element_type=f32)
    rest = jnp.dot(driver[:MEMBERS], lo, preferred_element_type=f32)
    return x + (both[:MEMBERS] + both[MEMBERS:] + rest)


def drivers_kernel(part_ref, weight_ref, terms_ref, place_ref, *refs):
    sources = refs[: 2 * GROUPS]
    lhs_ref, driver_ref, centre_ref, inverse_ref, z = refs[2 * GROUPS :]
    part = part_ref[0]
    for h in range(2):
        at = pl.multiple_of((part if h == 0 else 1 - part) * PART, 128)
        for p in range(GROUPS):
            src = sources[h * GROUPS + p]
            z[16 * p : 16 * p + 16, pl.ds(at, PART)] = src[0:16, :]
            z[64 + 4 * p : 68 + 4 * p, pl.ds(at, PART)] = src[16:20, :]
    for t in range(BLOCKS):
        begin = OBS + (t - 1) * POINTS * OBS
        if t == 0:
            prior = z[:, 0:OBS]
        else:
            prior = z[:, begin : begin + OBS] * weight_ref[t, 0:1, :]
            for k in range(1, POINTS):
                prior = prior + z[:, begin + k * OBS : begin + (k + 1) * OBS] * weight_ref[t, k : k + 1, :]
        value = terms_ref[t, 0:1, :]
        variance = terms_ref[t, 1:2, :]
        ybar = jnp.sum(prior, axis=0, keepdims=True) * f32(1.0 / MEMBERS)
        anomaly = prior - ybar
        spread = jnp.sum(anomaly * anomaly, axis=0, keepdims=True) * f32(1.0 / (MEMBERS - 1))
        gain = f32(1.0) / (spread + variance)
        shrink = -gain / (f32(1.0) + jnp.sqrt(variance * gain))
        coeff = gain * (value - ybar)
        driver = coeff + shrink * anomaly
        hi, lo = split((anomaly * f32(1.0 / (MEMBERS - 1))).T)
        lhs_ref[t] = jnp.concatenate([hi, hi, lo], axis=1)
        hi, lo = split(driver)
        driver_ref[t] = jnp.concatenate([hi, lo], axis=0)
        columns = terms_ref[t].T
        centre_ref[t] = jnp.broadcast_to(columns[:, 2:3], (OBS, 128))
        inverse_ref[t] = jnp.broadcast_to(columns[:, 3:4], (OBS, 128))
        if t < BLOCKS - 1:
            start = OBS + t * POINTS * OBS

            def step(i, carry):
                at = pl.multiple_of(start + i * TILE, 128)
                z[:, pl.ds(at, TILE)] = updated(
                    z[:, pl.ds(at, TILE)],
                    place_ref[:, pl.ds(at, TILE)],
                    lhs_ref[t],
                    driver_ref[t],
                    centre_ref[t],
                    inverse_ref[t],
                )
                return carry

            lax.fori_loop(0, (COLS - start) // TILE, step, 0)


def drivers(part, weight, terms, place, pieces):
    return pl.pallas_call(
        drivers_kernel,
        out_shape=[
            jax.ShapeDtypeStruct((BLOCKS, OBS, 3 * MEMBERS), bf16),
            jax.ShapeDtypeStruct((BLOCKS, 2 * MEMBERS, OBS), bf16),
            jax.ShapeDtypeStruct((BLOCKS, OBS, 128), f32),
            jax.ShapeDtypeStruct((BLOCKS, OBS, 128), f32),
        ],
        in_specs=[pl.BlockSpec(memory_space=pltpu.SMEM)] + whole(3 + 2 * GROUPS),
        out_specs=whole(4),
        scratch_shapes=[pltpu.VMEM((MEMBERS, COLS), f32)],
        compiler_params=params(),
        cost_estimate=pl.CostEstimate(flops=8 * 10**9, bytes_accessed=4 * 2**20, transcendentals=0),
        name="drivers",
    )(part, weight, terms, place, *pieces)


def update_kernel(first_ref, lhs_ref, driver_ref, centre_ref, inverse_ref, *refs):
    ins, outs = refs[:GROUPS], refs[GROUPS:]
    low = lax.broadcasted_iota(jnp.int32, (8, TILE), 0) < 4
    offsets = lax.broadcasted_iota(jnp.int32, (1, TILE), 1)
    first = first_ref[0]

    def join(a, b):
        return jnp.where(low, a, pltpu.roll(b, 4, 0)), jnp.where(low, pltpu.roll(a, 4, 0), b)

    def step(i, carry):
        at = i * TILE
        cols = [pl.ds(pl.multiple_of(base + at, 128), TILE) for base in (0, HALF, CHUNK, CHUNK + HALF, 2 * CHUNK)]
        rest = [ref[:, cols[4]] for ref in ins]
        pair = [join(rest[0], rest[1]), join(rest[2], rest[3])]
        xs = []
        for h in range(2):
            full = []
            for ref in ins:
                full += [ref[:, cols[h]], ref[:, cols[2 + h]]]
            xs.append(jnp.concatenate(full + [pair[0][h], pair[1][h]], axis=0))
        places = [(first + at + h * HALF + offsets).astype(f32) for h in range(2)]
        for t in range(BLOCKS):
            for h in range(2):
                xs[h] = updated(xs[h], places[h], lhs_ref[t], driver_ref[t], centre_ref[t], inverse_ref[t])
        for h in range(2):
            for p, ref in enumerate(outs):
                ref[:, cols[h]] = xs[h][16 * p : 16 * p + 8]
                ref[:, cols[2 + h]] = xs[h][16 * p + 8 : 16 * p + 16]
        for q in range(2):
            a, b = join(xs[0][64 + 8 * q : 72 + 8 * q], xs[1][64 + 8 * q : 72 + 8 * q])
            outs[2 * q][:, cols[4]] = a
            outs[2 * q + 1][:, cols[4]] = b
        return carry

    lax.fori_loop(0, HALF // TILE, step, 0)


def update(first, terms, pieces):
    return pl.pallas_call(
        update_kernel,
        out_shape=[jax.ShapeDtypeStruct((8, PACKED), f32)] * GROUPS,
        in_specs=[pl.BlockSpec(memory_space=pltpu.SMEM)] + whole(4 + GROUPS),
        out_specs=whole(GROUPS),
        compiler_params=params(),
        cost_estimate=pl.CostEstimate(flops=10 * 10**9, bytes_accessed=4 * 2**20, transcendentals=0),
        name="update",
    )(first, *terms, *pieces)


def unpack_kernel(chunk, rank_ref, *refs):
    pieces = refs[:GROUPS]
    out_ref, rows, sems = refs[-3:]
    rank = rank_ref[0]
    copies = []
    for d in range(GROUPS):
        src = pieces[d]
        rows[d, 0:8, :] = src[:, 0:CHUNK]
        rows[d, 8:16, :] = src[:, CHUNK : 2 * CHUNK]
        rows[d, 16:20, 0:HALF] = src[0:4, 2 * CHUNK : PACKED]
        rows[d, 16:20, HALF:CHUNK] = src[4:8, 2 * CHUNK : PACKED]
        at = pl.multiple_of(lax.rem(rank + d, GROUPS) * CELLS + chunk * CHUNK, 128)
        copy = pltpu.make_async_copy(rows.at[d], out_ref.at[:, pl.ds(at, CHUNK)], sems.at[d])
        copy.start()
        copies.append(copy)
    for copy in copies:
        copy.wait()


def unpack(chunk, rank, pieces, out):
    held = [] if out is None else [out]
    return pl.pallas_call(
        functools.partial(unpack_kernel, chunk),
        out_shape=jax.ShapeDtypeStruct((ROWS, GROUPS * CELLS), f32),
        in_specs=[pl.BlockSpec(memory_space=pltpu.SMEM)]
        + whole(GROUPS)
        + [pl.BlockSpec(memory_space=pl.ANY)] * len(held),
        out_specs=pl.BlockSpec(memory_space=pl.ANY),
        scratch_shapes=[pltpu.VMEM((GROUPS, ROWS, CHUNK), f32), pltpu.SemaphoreType.DMA((GROUPS,))],
        input_output_aliases={1 + GROUPS: 0} if held else {},
        compiler_params=params(),
        cost_estimate=pl.CostEstimate(flops=0, bytes_accessed=4 * 2**20, transcendentals=0),
        name="unpack",
    )(rank, *pieces, *held)


def shifted(x, axis, size, by):
    return lax.ppermute(x, axis, [(i, (i + by) % size) for i in range(size)])


def per_device(
    ensemble,
    block_order,
    obs_owner,
    interp_cells,
    interp_weight,
    obs_radius,
    obs_value,
    obs_variance,
):
    slabs = lax.axis_size("slab")
    member_rank = lax.axis_index("member")
    slab_rank = lax.axis_index("slab")
    here = slab_rank * GROUPS + member_rank
    rank = member_rank.reshape(1)
    part = (slab_rank % 2).reshape(1)

    pieces = pack(rank, ensemble)
    arrived = []
    for c in range(CHUNKS):
        arrived.append(
            [pieces[c]]
            + [shifted(pieces[d * CHUNKS + c], "member", GROUPS, d) for d in range(1, GROUPS)]
        )

    owner = obs_owner[block_order]
    cells = interp_cells.transpose(0, 2, 1)[block_order]
    weight = interp_weight.transpose(0, 2, 1)[block_order]
    everywhere = owner[:, None, :] * CELLS + cells
    local = everywhere - slab_rank * (GROUPS * CELLS)
    inside = (local >= 0) & (local < GROUPS * CELLS)
    place = jnp.where(inside, local, -1).reshape(-1)
    radius = obs_radius[block_order].astype(f32)
    zero = jnp.zeros_like(radius)
    terms = jnp.stack(
        [
            obs_value[block_order],
            obs_variance[block_order],
            everywhere[:, 0, :].astype(f32),
            1.0 / radius,
            zero,
            zero,
            zero,
            zero,
        ],
        axis=1,
    )
    columns = everywhere.astype(f32).reshape(1, -1)[:, POINTS * OBS - OBS :]

    keep, send = pick(place, part, weight[0], ensemble)
    chip = keep + lax.ppermute(send, "slab", [(i, i ^ 1) for i in range(slabs)])
    window = chip
    for by in (2, -2, 4, -4):
        window = window + shifted(chip, "slab", slabs, by)
    mine = [window] + [shifted(window, "member", GROUPS, d) for d in range(1, GROUPS)]
    other = [lax.ppermute(x, "slab", [(i, i ^ 1) for i in range(slabs)]) for x in mine]
    blocks = drivers(part, weight, terms, columns, mine + other)

    out = None
    for c in range(CHUNKS):
        first = (here * CELLS + c * CHUNK).reshape(1)
        new = update(first, blocks, arrived[c])
        back = [new[0]] + [shifted(new[d], "member", GROUPS, -d) for d in range(1, GROUPS)]
        out = unpack(c, rank, back, out)
    return out


def solution(mesh):
    in_specs = (P("member", "slab"), P(), P(), P(), P(), P(), P(), P())
    out_specs = P("member", "slab")
    return jax.shard_map(
        per_device, mesh=mesh, in_specs=in_specs, out_specs=out_specs, check_vma=False
    )
```

```python
import functools

import jax
import jax.numpy as jnp
from jax import lax
from jax.experimental import pallas as pl
from jax.experimental.pallas import tpu as pltpu
from jax.sharding import PartitionSpec as P

MEMBERS = 80
BLOCKS = 4
POINTS = 4
OBS = 256
GROUPS = 4
ROWS = MEMBERS // GROUPS
PADDED = 24
CELLS = 12288
CHUNKS = 4
EARLY = (0, 1, 2)
LATE = (3,)
PERMUTED = (1, 3)
CHUNK = CELLS // CHUNKS
HALF = CHUNK // 2
PACKED = 5 * HALF
COLS = OBS + (BLOCKS - 1) * POINTS * OBS
PART = COLS // 2
FAR = 128 + POINTS * 128
WIDE = 1024
UNROLL = 4
VMEM = 60 * 1024 * 1024

f32 = jnp.float32
bf16 = jnp.bfloat16


def split(x):
    hi = x.astype(bf16)
    lo = (x - hi.astype(f32)).astype(bf16)
    return hi, lo


def whole(n):
    return [pl.BlockSpec(memory_space=pltpu.VMEM)] * n


def smem(n):
    return [pl.BlockSpec(memory_space=pltpu.SMEM)] * n


def params():
    return pltpu.CompilerParams(vmem_limit_bytes=VMEM)


def cost(micros):
    return pl.CostEstimate(flops=0, bytes_accessed=int(micros * 1024), transcendentals=0)


def pack_kernel(ens_ref, *outs):
    for out_ref, chunks in zip(outs, (EARLY, LATE)):
        for q in range(GROUPS):
            for i, c in enumerate(chunks):
                o = i * PACKED
                at = q * CELLS + c * CHUNK
                mid = at + HALF
                out_ref[q, :, o : o + CHUNK] = ens_ref[0:8, at : at + CHUNK]
                out_ref[q, :, o + CHUNK : o + 2 * CHUNK] = ens_ref[8:16, at : at + CHUNK]
                out_ref[q, 0:4, o + 2 * CHUNK : o + PACKED] = ens_ref[16:20, at : at + HALF]
                out_ref[q, 4:8, o + 2 * CHUNK : o + PACKED] = ens_ref[16:20, mid : mid + HALF]


def pack(ensemble):
    return pl.pallas_call(
        pack_kernel,
        out_shape=[jax.ShapeDtypeStruct((GROUPS, 8, PACKED * len(c)), f32) for c in (EARLY, LATE)],
        in_specs=whole(1),
        out_specs=whole(2),
        compiler_params=params(),
        cost_estimate=cost(3),
        name="pack",
    )(ensemble)


def after_kernel(x_ref, first_ref, out_ref):
    pass


def after(x, first):
    anywhere = pl.BlockSpec(memory_space=pl.ANY)
    return pl.pallas_call(
        after_kernel,
        out_shape=jax.ShapeDtypeStruct(x.shape, x.dtype),
        in_specs=[anywhere, anywhere],
        out_specs=anywhere,
        input_output_aliases={0: 0},
        compiler_params=params(),
        cost_estimate=cost(1),
        name="after",
    )(x, first)


def pick_kernel(slab_ref, order_ref, owner_ref, cells_ref, weight_ref, ens_ref, after_ref, keep_ref, send_ref, held, *bufs):
    del after_ref
    slab = slab_ref[0]
    buf = bufs[POINTS]
    for point in bufs[:POINTS]:
        point[...] = jnp.zeros_like(point)

    blocks = [order_ref[t] for t in range(BLOCKS)]

    def scan(s, counts):
        counts = list(counts)
        for u in range(4):
            j = s * 4 + u
            for t in range(BLOCKS):
                held[t, counts[t]] = j
                counts[t] = counts[t] + jnp.where((owner_ref[blocks[t], j] >> 2) == slab, 1, 0)
        return tuple(counts)

    counts = lax.fori_loop(0, OBS // 4, scan, (jnp.int32(0),) * BLOCKS)
    lanes = lax.broadcasted_iota(jnp.int32, (8, 128), 1)
    lanes4 = lax.broadcasted_iota(jnp.int32, (4, 128), 1)
    for t in range(BLOCKS):
        count = counts[t]
        b = blocks[t]

        def some(s, carry):
            for u in range(UNROLL):
                i = s * UNROLL + u
                valid = i < count
                j = jnp.where(valid, held[t, i], 0)
                base = (owner_ref[b, j] & 3) * CELLS
                n = j & 127
                lane = jnp.where(valid, n, -1)
                hit = lanes == lane
                hit4 = lanes4 == lane
                dst = pl.ds(pl.multiple_of(t * OBS + (j - n), 128), 128)
                for k in range(POINTS):
                    point = bufs[k].at[u]
                    place = jnp.where(valid, base + cells_ref[b, k, j], 0)
                    src = pl.ds(pl.multiple_of((place >> 7) * 128, 128), 128)
                    shift = (n - place) & 127
                    point[0:8, dst] = jnp.where(hit, pltpu.roll(ens_ref[0:8, src], shift, 1), point[0:8, dst])
                    point[8:16, dst] = jnp.where(hit, pltpu.roll(ens_ref[8:16, src], shift, 1), point[8:16, dst])
                    point[16:20, dst] = jnp.where(hit4, pltpu.roll(ens_ref[16:20, src], shift, 1), point[16:20, dst])
            return carry

        lax.fori_loop(0, (count + UNROLL - 1) // UNROLL, some, 0)
    points = [sum(point[u] for u in range(1, UNROLL)) + point[0] for point in bufs[:POINTS]]
    weight = weight_ref[blocks[0]]
    total = points[0][:, 0:OBS] * weight[0:1, :]
    for k in range(1, POINTS):
        total = total + points[k][:, 0:OBS] * weight[k : k + 1, :]
    for h in range(2):
        half = slice(h * 128, h * 128 + 128)
        buf[h, :, 0:128] = total[:, half]
        for t in range(1, BLOCKS):
            for k in range(POINTS):
                o = 128 + ((t - 1) * POINTS + k) * 128
                at = t * OBS + h * 128
                buf[h, :, o : o + 128] = points[k][:, at : at + 128]
    part = lax.rem(slab, 2)
    keep_ref[...] = buf[part]
    send_ref[...] = buf[1 - part]


def pick(slab, order, owner, cells, weight, ensemble, after):
    return pl.pallas_call(
        pick_kernel,
        out_shape=[jax.ShapeDtypeStruct((PADDED, PART), f32)] * 2,
        in_specs=smem(4) + whole(2) + [pl.BlockSpec(memory_space=pl.ANY)],
        out_specs=whole(2),
        scratch_shapes=[pltpu.SMEM((BLOCKS, OBS + UNROLL), jnp.int32)]
        + [pltpu.VMEM((UNROLL, PADDED, BLOCKS * OBS), f32)] * POINTS
        + [pltpu.VMEM((2, PADDED, PART), f32)],
        compiler_params=params(),
        cost_estimate=cost(8),
        name="pick",
    )(slab, order, owner, cells, weight, ensemble, after)


def updated(x, place, lhs, driver, centre, inverse, slots):
    reps = x.shape[1] // 128
    mean = jnp.sum(x, axis=0, keepdims=True) * f32(1.0 / MEMBERS)
    hi, lo = split(x - mean)
    cov = jnp.dot(lhs, jnp.concatenate([hi, lo, hi], axis=0), preferred_element_type=f32)
    centre = jnp.concatenate([centre] * reps, axis=1)
    inverse = jnp.concatenate([inverse] * reps, axis=1)
    loc = jnp.maximum(f32(0.0), f32(1.0) - jnp.abs(place - centre) * inverse)
    hi, lo = split(loc * cov)
    if slots == 64:
        return x + jnp.dot(driver, jnp.concatenate([hi, lo, hi], axis=0), preferred_element_type=f32)
    if slots == 128:
        both = jnp.dot(driver, jnp.concatenate([hi, lo], axis=0), preferred_element_type=f32)
        return x + (both[:MEMBERS] + both[MEMBERS:])
    both = jnp.dot(driver, hi, preferred_element_type=f32)
    rest = jnp.dot(driver[:MEMBERS], lo, preferred_element_type=f32)
    return x + (both[:MEMBERS] + both[MEMBERS:] + rest)


def drivers_kernel(here_ref, order_ref, owner_ref, cells_ref, weight_ref, radius_ref, value_ref, variance_ref, *refs):
    mine_ref, other_ref = refs[:2]
    count_ref, lhs_ref, driver_ref, centre_ref, inverse_ref, z, place, full, whole_lhs, wide = refs[2:]
    here = here_ref[0]
    part = lax.rem(here // GROUPS, 2)
    for src, h in ((mine_ref, part), (other_ref, 1 - part)):
        for p in range(GROUPS):
            for i in range(PART // 128):
                cols = slice(i * 128, i * 128 + 128)
                at = pl.ds(pl.multiple_of(i * OBS + h * 128, 128), 128)
                z[16 * p : 16 * p + 16, at] = src[PADDED * p : PADDED * p + 16, cols]
                z[64 + 4 * p : 68 + 4 * p, at] = src[PADDED * p + 16 : PADDED * p + 20, cols]
    slot = lax.broadcasted_iota(jnp.int32, (OBS, OBS), 0)
    column = lax.broadcasted_iota(jnp.int32, (OBS, OBS), 1)
    before = jnp.where(slot < column, f32(1.0), f32(0.0)).astype(bf16)
    begin = (here * CELLS).astype(f32)
    end = begin + f32(CELLS - 1)

    for t in range(BLOCKS):
        b = order_ref[t]
        everywhere = (owner_ref[pl.ds(b, 1), :] * CELLS + cells_ref[b]).astype(f32)
        if t > 0:
            for k in range(POINTS):
                o = OBS + (t - 1) * POINTS * OBS + k * OBS
                place[:, o : o + OBS] = everywhere[k : k + 1, :]

    for t in range(BLOCKS):
        b = order_ref[t]
        start = OBS + (t - 1) * POINTS * OBS
        weight = weight_ref[b]
        if t == 0:
            prior = z[:, 0:OBS]
        else:
            prior = z[:, start : start + OBS] * weight[0:1, :]
            for k in range(1, POINTS):
                prior = prior + z[:, start + k * OBS : start + (k + 1) * OBS] * weight[k : k + 1, :]
        value = value_ref[pl.ds(b, 1), :]
        variance = variance_ref[pl.ds(b, 1), :]
        centre = (owner_ref[pl.ds(b, 1), :] * CELLS + cells_ref[b, 0:1, :]).astype(f32)
        radius = radius_ref[pl.ds(b, 1), :].astype(f32)
        inverse = f32(1.0) / radius
        ybar = jnp.sum(prior, axis=0, keepdims=True) * f32(1.0 / MEMBERS)
        anomaly = prior - ybar
        spread = jnp.sum(anomaly * anomaly, axis=0, keepdims=True) * f32(1.0 / (MEMBERS - 1))
        gain = f32(1.0) / (spread + variance)
        shrink = -gain / (f32(1.0) + jnp.sqrt(variance * gain))
        coeff = gain * (value - ybar)
        driver = coeff + shrink * anomaly
        hi, lo = split((anomaly * f32(1.0 / (MEMBERS - 1))).T)
        lhs = jnp.concatenate([hi, hi, lo], axis=1)
        dhi, dlo = split(driver)
        both = jnp.concatenate([dhi, dlo], axis=0)

        if t < BLOCKS - 1:
            terms = jnp.concatenate([centre, inverse, jnp.zeros((6, OBS), f32)], axis=0).T
            whole_lhs[...] = lhs
            full[...] = both
            wide[0] = jnp.broadcast_to(terms[:, 0:1], (OBS, 128))
            wide[1] = jnp.broadcast_to(terms[:, 1:2], (OBS, 128))

            def evolve(i, carry):
                cols = pl.ds(pl.multiple_of(OBS + i * WIDE, 128), WIDE)
                z[:, cols] = updated(z[:, cols], place[:, cols], whole_lhs[...], full[...], wide[0], wide[1], OBS)
                return carry

            lax.fori_loop(t * POINTS * OBS // WIDE, (BLOCKS - 1) * POINTS * OBS // WIDE, evolve, 0)

        away = jnp.maximum(jnp.maximum(begin - centre, centre - end), f32(0.0))
        active = jnp.where(away < radius, f32(1.0), f32(0.0))
        count = jnp.sum(active).astype(jnp.int32)
        count_ref[t] = count
        ahead = jnp.dot(jnp.broadcast_to(active, (8, OBS)).astype(bf16), before, preferred_element_type=f32)
        index = jnp.where(active > 0, ahead[0:1, :], f32(-1.0)).astype(jnp.int32)
        hit = index == slot
        chosen = jnp.where(hit, f32(1.0), f32(0.0)).astype(bf16)
        lhs_ref[t] = jnp.dot(chosen, lhs, preferred_element_type=f32).astype(bf16)
        centre_ref[t] = jnp.broadcast_to(jnp.sum(jnp.where(hit, centre, f32(0.0)), axis=1, keepdims=True), (OBS, 128))
        inverse_ref[t] = jnp.broadcast_to(jnp.sum(jnp.where(hit, inverse, f32(0.0)), axis=1, keepdims=True), (OBS, 128))
        nt = (((1,), (1,)), ((), ()))

        @pl.when(count <= 64)
        def _():
            again = jnp.where(index == (slot & 63), f32(1.0), f32(0.0)).astype(bf16)
            kept = lax.dot_general(both, again, nt, preferred_element_type=f32)
            lane = lax.broadcasted_iota(jnp.int32, (MEMBERS, OBS), 1)
            driver_ref[t, 0:MEMBERS] = jnp.where(lane < 128, kept[:MEMBERS], kept[MEMBERS:]).astype(bf16)

        @pl.when(count > 64)
        def _():
            kept = lax.dot_general(both, chosen, nt, preferred_element_type=f32).astype(bf16)
            driver_ref[t] = kept

            @pl.when(count <= 128)
            def _():
                driver_ref[t, 0:MEMBERS, 128:256] = kept[:MEMBERS, 0:128]
                driver_ref[t, MEMBERS : 2 * MEMBERS, 128:256] = jnp.zeros((MEMBERS, 128), bf16)


def drivers(here, order, owner, cells, weight, radius, value, variance, mine, other):
    return pl.pallas_call(
        drivers_kernel,
        out_shape=[
            jax.ShapeDtypeStruct((BLOCKS,), jnp.int32),
            jax.ShapeDtypeStruct((BLOCKS, OBS, 3 * MEMBERS), bf16),
            jax.ShapeDtypeStruct((BLOCKS, 2 * MEMBERS, OBS), bf16),
            jax.ShapeDtypeStruct((BLOCKS, OBS, 128), f32),
            jax.ShapeDtypeStruct((BLOCKS, OBS, 128), f32),
        ],
        in_specs=smem(2) + whole(8),
        out_specs=smem(1) + whole(4),
        scratch_shapes=[
            pltpu.VMEM((MEMBERS, COLS), f32),
            pltpu.VMEM((1, COLS), f32),
            pltpu.VMEM((2 * MEMBERS, OBS), bf16),
            pltpu.VMEM((OBS, 3 * MEMBERS), bf16),
            pltpu.VMEM((2, OBS, 128), f32),
        ],
        compiler_params=params(),
        cost_estimate=cost(8),
        name="drivers",
    )(here, order, owner, cells, weight, radius, value, variance, mine, other)


def update_kernel(chunk, apart, here_ref, count_ref, lhs_ref, driver_ref, centre_ref, inverse_ref, *refs):
    in_ref, x = refs[0], refs[-1]
    out_ref = refs[-2] if apart else refs[1]
    ins = [in_ref.at[q] for q in range(GROUPS)]
    outs = [out_ref.at[q] for q in range(GROUPS)]
    low = lax.broadcasted_iota(jnp.int32, (8, HALF), 0) < 4
    offsets = lax.broadcasted_iota(jnp.int32, (1, HALF), 1)
    first = here_ref[0] * CELLS + chunk * CHUNK

    def join(a, b):
        return jnp.where(low, a, pltpu.roll(b, 4, 0)), jnp.where(low, pltpu.roll(a, 4, 0), b)

    for p, ref in enumerate(ins):
        for h in range(2):
            x[h, 16 * p : 16 * p + 8] = ref[:, h * HALF : (h + 1) * HALF]
            x[h, 16 * p + 8 : 16 * p + 16] = ref[:, CHUNK + h * HALF : CHUNK + (h + 1) * HALF]
    for q in range(2):
        rest = join(ins[2 * q][:, 2 * CHUNK : PACKED], ins[2 * q + 1][:, 2 * CHUNK : PACKED])
        for h in range(2):
            x[h, 64 + 8 * q : 72 + 8 * q] = rest[h]

    def block(t, carry):
        count = count_ref[t]

        def apply(slots):
            width = 192 if slots == 64 else OBS
            height = MEMBERS if slots == 64 else 2 * MEMBERS
            lhs = lhs_ref[t, 0:slots]
            driver = driver_ref[t, 0:height, 0:width]
            for h in range(2):
                place = (first + h * HALF + offsets).astype(f32)
                x[h] = updated(x[h], place, lhs, driver, centre_ref[t, 0:slots], inverse_ref[t, 0:slots], slots)

        @pl.when((count > 0) & (count <= 64))
        def _():
            apply(64)

        @pl.when((count > 64) & (count <= 128))
        def _():
            apply(128)

        @pl.when(count > 128)
        def _():
            apply(OBS)

        return carry

    lax.fori_loop(0, BLOCKS, block, 0)
    for p, ref in enumerate(outs):
        for h in range(2):
            ref[:, h * HALF : (h + 1) * HALF] = x[h, 16 * p : 16 * p + 8]
            ref[:, CHUNK + h * HALF : CHUNK + (h + 1) * HALF] = x[h, 16 * p + 8 : 16 * p + 16]
    for q in range(2):
        a, b = join(x[0, 64 + 8 * q : 72 + 8 * q], x[1, 64 + 8 * q : 72 + 8 * q])
        outs[2 * q][:, 2 * CHUNK : PACKED] = a
        outs[2 * q + 1][:, 2 * CHUNK : PACKED] = b
    if apart:
        for d in range(GROUPS):
            refs[1 + d][...] = out_ref[lax.rem(here_ref[0] + d, GROUPS)]


def fixed(shape, index):
    return pl.BlockSpec(shape, lambda i: index, pipeline_mode=pl.Buffered(1))


def update(chunk, apart, index, here, terms, arrived):
    gathered = (GROUPS, 8, PACKED)
    shapes = [gathered[1:]] * GROUPS if apart else [gathered]
    return pl.pallas_call(
        functools.partial(update_kernel, chunk, apart),
        grid=(1,),
        out_shape=[jax.ShapeDtypeStruct(shape, f32) for shape in shapes],
        in_specs=smem(2)
        + [fixed(a.shape, (0, 0, 0)) for a in terms[1:]]
        + [fixed((GROUPS, 8, PACKED), (0, 0, index))],
        out_specs=[fixed(shape, (0,) * len(shape)) for shape in shapes],
        scratch_shapes=[pltpu.VMEM(gathered, f32)] * apart
        + [pltpu.VMEM((2, MEMBERS, HALF), f32)],
        compiler_params=params(),
        cost_estimate=cost(8),
        name="update",
    )(here, *terms, arrived)


def unpack_kernel(chunk, apart, rank_ref, *refs):
    out_ref, rows, sems = refs[-3:]
    copies = []
    for i in range(GROUPS):
        src = refs[i] if apart else refs[0].at[i]
        quarter = lax.rem(rank_ref[0] + GROUPS - i, GROUPS) if apart else i
        rows[i, 0:8, :] = src[:, 0:CHUNK]
        rows[i, 8:16, :] = src[:, CHUNK : 2 * CHUNK]
        rows[i, 16:20, 0:HALF] = src[0:4, 2 * CHUNK : PACKED]
        rows[i, 16:20, HALF:CHUNK] = src[4:8, 2 * CHUNK : PACKED]
        at = pl.multiple_of(quarter * CELLS + chunk * CHUNK, 128)
        copy = pltpu.make_async_copy(rows.at[i], out_ref.at[:, pl.ds(at, CHUNK)], sems.at[i])
        copy.start()
        copies.append(copy)
    for copy in copies:
        copy.wait()


def unpack(chunk, apart, rank, pieces, out):
    held = [] if out is None else [out]
    return pl.pallas_call(
        functools.partial(unpack_kernel, chunk, apart),
        out_shape=jax.ShapeDtypeStruct((ROWS, GROUPS * CELLS), f32),
        in_specs=smem(1) + whole(len(pieces)) + [pl.BlockSpec(memory_space=pl.ANY)] * len(held),
        out_specs=pl.BlockSpec(memory_space=pl.ANY),
        scratch_shapes=[pltpu.VMEM((GROUPS, ROWS, CHUNK), f32), pltpu.SemaphoreType.DMA((GROUPS,))],
        input_output_aliases={1 + len(pieces): 0} if held else {},
        compiler_params=params(),
        cost_estimate=cost(2),
        name="unpack",
    )(rank, *pieces, *held)


def shifted(x, axis, size, by):
    return lax.ppermute(x, axis, [(i, (i + by) % size) for i in range(size)])


def exchanged(x):
    return lax.all_to_all(x, "member", split_axis=0, concat_axis=0, tiled=True)


def per_device(
    ensemble,
    block_order,
    obs_owner,
    interp_cells,
    interp_weight,
    obs_radius,
    obs_value,
    obs_variance,
):
    slabs = lax.axis_size("slab")
    member_rank = lax.axis_index("member")
    slab_rank = lax.axis_index("slab")
    rank = member_rank.reshape(1)
    slab = slab_rank.reshape(1)
    here = slab * GROUPS + rank

    early, late = pack(ensemble)
    arrived = [exchanged(early)]

    cells = interp_cells.transpose(0, 2, 1)
    weight = interp_weight.transpose(0, 2, 1)
    keep, send = pick(slab, block_order, obs_owner, cells, weight, ensemble, early)
    chip = keep + lax.ppermute(send, "slab", [(i, i ^ 1) for i in range(slabs)])
    near = chip + shifted(chip, "slab", slabs, 2) + shifted(chip, "slab", slabs, -2)
    far = shifted(chip[:, :FAR], "slab", slabs, 4) + shifted(chip[:, :FAR], "slab", slabs, -4)
    window = jnp.concatenate([near[:, :FAR] + far, near[:, FAR:]], axis=1)
    mine = lax.all_gather(after(window, arrived[0]), "member", axis=0, tiled=True)
    other = lax.ppermute(mine, "slab", [(i, i ^ 1) for i in range(slabs)])
    arrived.append(exchanged(after(late, other)))
    terms = drivers(
        here, block_order, obs_owner, cells, weight, obs_radius, obs_value, obs_variance, mine, other
    )

    out = None
    for c in range(CHUNKS):
        group, index = (0, EARLY.index(c)) if c in EARLY else (1, LATE.index(c))
        apart = c in PERMUTED
        new = update(c, apart, index, here, terms, arrived[group])
        if c == 0:
            new = [after(new[0], arrived[1])]
        if apart:
            back = [new[0]] + [shifted(new[d], "member", GROUPS, d) for d in range(1, GROUPS)]
        else:
            back = [exchanged(new[0])]
        out = unpack(c, apart, rank, back, out)
    return out


def solution(mesh):
    in_specs = (P("member", "slab"), P(), P(), P(), P(), P(), P(), P())
    out_specs = P("member", "slab")
    return jax.shard_map(
        per_device, mesh=mesh, in_specs=in_specs, out_specs=out_specs, check_vma=False
    )
```

```python
import functools

import jax
import jax.numpy as jnp
from jax import lax
from jax.experimental import pallas as pl
from jax.experimental.pallas import tpu as pltpu
from jax.sharding import PartitionSpec as P

MEMBERS = 80
BLOCKS = 4
POINTS = 4
OBS = 256
GROUPS = 4
ROWS = MEMBERS // GROUPS
PADDED = 24
CELLS = 12288
CHUNKS = 4
EARLY = (0, 1)
LATE = (2, 3)
PERMUTED = (1, 3)
CHUNK = CELLS // CHUNKS
HALF = CHUNK // 2
PACKED = 5 * HALF
COLS = OBS + (BLOCKS - 1) * POINTS * OBS
PART = COLS // 2
FAR = 128 + POINTS * 128
WIDE = 1024
UNROLL = 4
MIB = 1024 * 1024

f32 = jnp.float32
bf16 = jnp.bfloat16


def split(x):
    hi = x.astype(bf16)
    lo = (x - hi.astype(f32)).astype(bf16)
    return hi, lo


def whole(n):
    return [pl.BlockSpec(memory_space=pltpu.VMEM)] * n


def smem(n):
    return [pl.BlockSpec(memory_space=pltpu.SMEM)] * n


def params(mib):
    return pltpu.CompilerParams(vmem_limit_bytes=mib * MIB)


def cost(micros):
    return pl.CostEstimate(flops=0, bytes_accessed=int(micros * 1024), transcendentals=0)


def place_piece(out, o, ens_ref, c):
    at, mid = c * CHUNK, c * CHUNK + HALF
    out[:, o : o + CHUNK] = ens_ref[0:8, at : at + CHUNK]
    out[:, o + CHUNK : o + 2 * CHUNK] = ens_ref[8:16, at : at + CHUNK]
    out[0:4, o + 2 * CHUNK : o + PACKED] = ens_ref[16:20, at : at + HALF]
    out[4:8, o + 2 * CHUNK : o + PACKED] = ens_ref[16:20, mid : mid + HALF]


def pack_kernel(rank_ref, slab_ref, order_ref, owner_ref, ens_ref, early_ref, *refs):
    late_refs, lists_ref, owners = refs[:GROUPS], refs[GROUPS], refs[GROUPS + 1]
    step = pl.program_id(0)

    @pl.when(step == 1)
    def _():
        owners[...] = jnp.full_like(owners, -1)
        for t in range(BLOCKS):
            owners[t : t + 1, :] = owner_ref[pl.ds(order_ref[t], 1), :]
        row = lax.broadcasted_iota(jnp.int32, (OBS, OBS), 0)
        column = lax.broadcasted_iota(jnp.int32, (OBS, OBS), 1)
        before = jnp.where(row < column, f32(1.0), f32(0.0)).astype(bf16)
        inside = (owners[...] >> 2) == slab_ref[0]
        ahead = jnp.dot(jnp.where(inside, f32(1.0), f32(0.0)).astype(bf16), before, preferred_element_type=f32)
        index = jnp.where(inside, ahead, f32(-1.0)).T
        for t in range(BLOCKS):
            hit = index[:, t : t + 1] == column.astype(f32)
            held = jnp.sum(jnp.where(hit, row.astype(f32), f32(0.0)), axis=0, keepdims=True)
            lists_ref[t : t + 1, :] = held.astype(jnp.int32)
        total = jnp.sum(jnp.where(inside, f32(1.0), f32(0.0)), axis=1, keepdims=True)
        lists_ref[BLOCKS : 2 * BLOCKS, :] = jnp.broadcast_to(total[0:BLOCKS], (BLOCKS, OBS)).astype(jnp.int32)

    for i, c in enumerate(EARLY):
        place_piece(early_ref.at[0], i * PACKED, ens_ref, c)
    for d in range(GROUPS):

        @pl.when(step == d)
        def _():
            for i, c in enumerate(LATE):
                place_piece(late_refs[d], i * PACKED, ens_ref, c)


def pack(rank, slab, order, owner, ensemble):
    late = jax.ShapeDtypeStruct((8, PACKED * len(LATE)), f32)

    def quarter(i, rank_ref):
        return lax.rem(rank_ref[0] + i, GROUPS)

    return pl.pallas_call(
        pack_kernel,
        grid_spec=pltpu.PrefetchScalarGridSpec(
            num_scalar_prefetch=3,
            grid=(GROUPS,),
            in_specs=[
                pl.BlockSpec((BLOCKS, OBS), lambda i, *_: (0, 0)),
                pl.BlockSpec((ROWS, CELLS), lambda i, r, *_: (0, quarter(i, r))),
            ],
            out_specs=[pl.BlockSpec((1, 8, PACKED * len(EARLY)), lambda i, r, *_: (quarter(i, r), 0, 0))]
            + [pl.BlockSpec(late.shape, lambda i, *_: (0, 0))] * GROUPS
            + [pl.BlockSpec((2 * BLOCKS, OBS), lambda i, *_: (0, 0))],
            scratch_shapes=[pltpu.VMEM((2 * BLOCKS, OBS), jnp.int32)],
        ),
        out_shape=[jax.ShapeDtypeStruct((GROUPS, 8, PACKED * len(EARLY)), f32)]
        + [late] * GROUPS
        + [jax.ShapeDtypeStruct((2 * BLOCKS, OBS), jnp.int32)],
        compiler_params=params(60),
        cost_estimate=cost(3),
        name="pack",
    )(rank, slab, order, owner, ensemble)


def after_kernel(*refs):
    pass


def after(xs, *firsts):
    anywhere = pl.BlockSpec(memory_space=pl.ANY)
    n = len(xs)
    return pl.pallas_call(
        after_kernel,
        out_shape=[jax.ShapeDtypeStruct(x.shape, x.dtype) for x in xs],
        in_specs=[anywhere] * (n + len(firsts)),
        out_specs=[anywhere] * n,
        input_output_aliases={i: i for i in range(n)},
        compiler_params=params(60),
        cost_estimate=cost(1),
        name="after",
    )(*xs, *firsts)


def pick_kernel(slab_ref, order_ref, owner_ref, cells_ref, held, weight_ref, ens_ref, after_ref, keep_ref, send_ref, *bufs):
    del after_ref
    slab = slab_ref[0]
    buf = bufs[POINTS]
    for point in bufs[:POINTS]:
        point[...] = jnp.zeros_like(point)

    blocks = [order_ref[t] for t in range(BLOCKS)]
    lanes = lax.broadcasted_iota(jnp.int32, (8, 128), 1)
    lanes4 = lax.broadcasted_iota(jnp.int32, (4, 128), 1)
    for t in range(BLOCKS):
        count = held[BLOCKS + t, 0]
        b = blocks[t]

        def some(s, carry):
            for u in range(UNROLL):
                i = s * UNROLL + u
                valid = i < count
                j = jnp.where(valid, held[t, i], 0)
                base = (owner_ref[b, j] & 3) * CELLS
                n = j & 127
                lane = jnp.where(valid, n, -1)
                hit = lanes == lane
                hit4 = lanes4 == lane
                dst = pl.ds(pl.multiple_of(t * OBS + (j - n), 128), 128)
                for k in range(POINTS):
                    point = bufs[k].at[u]
                    place = jnp.where(valid, base + cells_ref[b, k, j], 0)
                    src = pl.ds(pl.multiple_of((place >> 7) * 128, 128), 128)
                    shift = (n - place) & 127
                    point[0:8, dst] = jnp.where(hit, pltpu.roll(ens_ref[0:8, src], shift, 1), point[0:8, dst])
                    point[8:16, dst] = jnp.where(hit, pltpu.roll(ens_ref[8:16, src], shift, 1), point[8:16, dst])
                    point[16:20, dst] = jnp.where(hit4, pltpu.roll(ens_ref[16:20, src], shift, 1), point[16:20, dst])
            return carry

        lax.fori_loop(0, (count + UNROLL - 1) // UNROLL, some, 0)
    points = [sum(point[u] for u in range(1, UNROLL)) + point[0] for point in bufs[:POINTS]]
    weight = weight_ref[blocks[0]]
    total = points[0][:, 0:OBS] * weight[0:1, :]
    for k in range(1, POINTS):
        total = total + points[k][:, 0:OBS] * weight[k : k + 1, :]
    for h in range(2):
        half = slice(h * 128, h * 128 + 128)
        buf[h, :, 0:128] = total[:, half]
        for t in range(1, BLOCKS):
            for k in range(POINTS):
                o = 128 + ((t - 1) * POINTS + k) * 128
                at = t * OBS + h * 128
                buf[h, :, o : o + 128] = points[k][:, at : at + 128]
    part = lax.rem(slab, 2)
    keep_ref[...] = buf[part]
    send_ref[...] = buf[1 - part]


def pick(slab, order, owner, cells, lists, weight, ensemble, after):
    return pl.pallas_call(
        pick_kernel,
        out_shape=[jax.ShapeDtypeStruct((PADDED, PART), f32)] * 2,
        in_specs=smem(5) + whole(2) + [pl.BlockSpec(memory_space=pl.ANY)],
        out_specs=whole(2),
        scratch_shapes=[pltpu.VMEM((UNROLL, PADDED, BLOCKS * OBS), f32)] * POINTS
        + [pltpu.VMEM((2, PADDED, PART), f32)],
        compiler_params=params(60),
        cost_estimate=cost(8),
        name="pick",
    )(slab, order, owner, cells, lists, weight, ensemble, after)


def window_kernel(chip_ref, *refs):
    near, far, out_ref = refs[0:2], refs[2:4], refs[-1]
    total = chip_ref[...] + near[0][...] + near[1][...]
    out_ref[:, 0:FAR] = total[:, 0:FAR] + far[0][...] + far[1][...]
    out_ref[:, FAR:PART] = total[:, FAR:PART]


def window(chip, near, far, firsts):
    return pl.pallas_call(
        window_kernel,
        out_shape=jax.ShapeDtypeStruct((PADDED, PART), f32),
        in_specs=whole(5) + [pl.BlockSpec(memory_space=pl.ANY)] * len(firsts),
        out_specs=pl.BlockSpec(memory_space=pltpu.VMEM),
        compiler_params=params(4),
        cost_estimate=cost(1),
        name="window",
    )(chip, *near, *far, *firsts)


def reach_kernel(here_ref, order_ref, owner_ref, cells_ref, radius_ref, after_ref, *refs):
    del after_ref
    count_ref, index_ref, chosen_ref, centre_ref, inverse_ref, wide_ref, place = refs
    slot = lax.broadcasted_iota(jnp.int32, (OBS, OBS), 0)
    column = lax.broadcasted_iota(jnp.int32, (OBS, OBS), 1)
    before = jnp.where(slot < column, f32(1.0), f32(0.0)).astype(bf16)
    begin = (here_ref[0] * CELLS).astype(f32)
    end = begin + f32(CELLS - 1)
    place[:, 0:OBS] = jnp.zeros((1, OBS), f32)
    for t in range(BLOCKS):
        b = order_ref[t]
        everywhere = (owner_ref[pl.ds(b, 1), :] * CELLS + cells_ref[b]).astype(f32)
        if t > 0:
            for k in range(POINTS):
                o = OBS + (t - 1) * POINTS * OBS + k * OBS
                place[:, o : o + OBS] = everywhere[k : k + 1, :]
        centre = everywhere[0:1, :]
        radius = radius_ref[pl.ds(b, 1), :].astype(f32)
        inverse = f32(1.0) / radius
        terms = jnp.concatenate([centre, inverse, jnp.zeros((6, OBS), f32)], axis=0).T
        wide_ref[t, 0] = jnp.broadcast_to(terms[:, 0:1], (OBS, 128))
        wide_ref[t, 1] = jnp.broadcast_to(terms[:, 1:2], (OBS, 128))
        away = jnp.maximum(jnp.maximum(begin - centre, centre - end), f32(0.0))
        active = jnp.where(away < radius, f32(1.0), f32(0.0))
        count_ref[t] = jnp.sum(active).astype(jnp.int32)
        ahead = jnp.dot(jnp.broadcast_to(active, (8, OBS)).astype(bf16), before, preferred_element_type=f32)
        index = jnp.where(active > 0, ahead[0:1, :], f32(-1.0)).astype(jnp.int32)
        index_ref[t] = index
        hit = index == slot
        chosen_ref[t] = jnp.where(hit, f32(1.0), f32(0.0)).astype(bf16)
        centre_ref[t] = jnp.broadcast_to(jnp.sum(jnp.where(hit, centre, f32(0.0)), axis=1, keepdims=True), (OBS, 128))
        inverse_ref[t] = jnp.broadcast_to(jnp.sum(jnp.where(hit, inverse, f32(0.0)), axis=1, keepdims=True), (OBS, 128))


def reach(here, order, owner, cells, radius, first):
    shape = jax.ShapeDtypeStruct
    return pl.pallas_call(
        reach_kernel,
        out_shape=[
            shape((BLOCKS,), jnp.int32),
            shape((BLOCKS, 1, OBS), jnp.int32),
            shape((BLOCKS, OBS, OBS), bf16),
            shape((BLOCKS, OBS, 128), f32),
            shape((BLOCKS, OBS, 128), f32),
            shape((BLOCKS, 2, OBS, 128), f32),
            shape((1, COLS), f32),
        ],
        in_specs=smem(2) + whole(3) + [pl.BlockSpec(memory_space=pl.ANY)],
        out_specs=smem(1) + whole(6),
        compiler_params=params(60),
        cost_estimate=cost(2),
        name="reach",
    )(here, order, owner, cells, radius, first)


def updated(x, place, lhs, driver, centre, inverse, slots):
    reps = x.shape[1] // 128
    mean = jnp.sum(x, axis=0, keepdims=True) * f32(1.0 / MEMBERS)
    hi, lo = split(x - mean)
    cov = jnp.dot(lhs, jnp.concatenate([hi, lo, hi], axis=0), preferred_element_type=f32)
    centre = jnp.concatenate([centre] * reps, axis=1)
    inverse = jnp.concatenate([inverse] * reps, axis=1)
    loc = jnp.maximum(f32(0.0), f32(1.0) - jnp.abs(place - centre) * inverse)
    hi, lo = split(loc * cov)
    if slots == 64:
        return x + jnp.dot(driver, jnp.concatenate([hi, lo, hi], axis=0), preferred_element_type=f32)
    if slots == 128:
        both = jnp.dot(driver, jnp.concatenate([hi, lo], axis=0), preferred_element_type=f32)
        return x + (both[:MEMBERS] + both[MEMBERS:])
    both = jnp.dot(driver, hi, preferred_element_type=f32)
    rest = jnp.dot(driver[:MEMBERS], lo, preferred_element_type=f32)
    return x + (both[:MEMBERS] + both[MEMBERS:] + rest)


def drivers_kernel(here_ref, order_ref, count_ref, *refs):
    weight_ref, value_ref, variance_ref, index_ref, chosen_ref, wide, place, mine_ref, other_ref = refs[:9]
    lhs_ref, driver_ref, z, full, whole_lhs = refs[9:]
    part = lax.rem(here_ref[0] // GROUPS, 2)
    for src, h in ((mine_ref, part), (other_ref, 1 - part)):
        for p in range(GROUPS):
            for i in range(PART // 128):
                cols = slice(i * 128, i * 128 + 128)
                at = pl.ds(pl.multiple_of(i * OBS + h * 128, 128), 128)
                z[16 * p : 16 * p + 16, at] = src[PADDED * p : PADDED * p + 16, cols]
                z[64 + 4 * p : 68 + 4 * p, at] = src[PADDED * p + 16 : PADDED * p + 20, cols]

    for t in range(BLOCKS):
        b = order_ref[t]
        start = OBS + (t - 1) * POINTS * OBS
        weight = weight_ref[b]
        if t == 0:
            prior = z[:, 0:OBS]
        else:
            prior = z[:, start : start + OBS] * weight[0:1, :]
            for k in range(1, POINTS):
                prior = prior + z[:, start + k * OBS : start + (k + 1) * OBS] * weight[k : k + 1, :]
        value = value_ref[pl.ds(b, 1), :]
        variance = variance_ref[pl.ds(b, 1), :]
        ybar = jnp.sum(prior, axis=0, keepdims=True) * f32(1.0 / MEMBERS)
        anomaly = prior - ybar
        spread = jnp.sum(anomaly * anomaly, axis=0, keepdims=True) * f32(1.0 / (MEMBERS - 1))
        gain = f32(1.0) / (spread + variance)
        shrink = -gain / (f32(1.0) + jnp.sqrt(variance * gain))
        coeff = gain * (value - ybar)
        driver = coeff + shrink * anomaly
        hi, lo = split((anomaly * f32(1.0 / (MEMBERS - 1))).T)
        lhs = jnp.concatenate([hi, hi, lo], axis=1)
        dhi, dlo = split(driver)
        both = jnp.concatenate([dhi, dlo], axis=0)

        if t < BLOCKS - 1:
            whole_lhs[...] = lhs
            full[...] = both

            def evolve(i, carry):
                cols = pl.ds(pl.multiple_of(OBS + i * WIDE, 128), WIDE)
                z[:, cols] = updated(z[:, cols], place[:, cols], whole_lhs[...], full[...], wide[t, 0], wide[t, 1], OBS)
                return carry

            lax.fori_loop(t * POINTS * OBS // WIDE, (BLOCKS - 1) * POINTS * OBS // WIDE, evolve, 0)

        count = count_ref[t]
        lhs_ref[t] = jnp.dot(chosen_ref[t], lhs, preferred_element_type=f32).astype(bf16)
        nt = (((1,), (1,)), ((), ()))

        @pl.when(count <= 64)
        def _():
            slot = lax.broadcasted_iota(jnp.int32, (OBS, OBS), 0)
            again = jnp.where(index_ref[t] == (slot & 63), f32(1.0), f32(0.0)).astype(bf16)
            kept = lax.dot_general(both, again, nt, preferred_element_type=f32)
            lane = lax.broadcasted_iota(jnp.int32, (MEMBERS, OBS), 1)
            driver_ref[t, 0:MEMBERS] = jnp.where(lane < 128, kept[:MEMBERS], kept[MEMBERS:]).astype(bf16)

        @pl.when(count > 64)
        def _():
            kept = lax.dot_general(both, chosen_ref[t], nt, preferred_element_type=f32).astype(bf16)
            driver_ref[t] = kept

            @pl.when(count <= 128)
            def _():
                driver_ref[t, 0:MEMBERS, 128:256] = kept[:MEMBERS, 0:128]
                driver_ref[t, MEMBERS : 2 * MEMBERS, 128:256] = jnp.zeros((MEMBERS, 128), bf16)


def drivers(here, order, count, weight, value, variance, index, chosen, wide, place, mine, other):
    return pl.pallas_call(
        drivers_kernel,
        out_shape=[
            jax.ShapeDtypeStruct((BLOCKS, OBS, 3 * MEMBERS), bf16),
            jax.ShapeDtypeStruct((BLOCKS, 2 * MEMBERS, OBS), bf16),
        ],
        in_specs=smem(3) + whole(9),
        out_specs=whole(2),
        scratch_shapes=[
            pltpu.VMEM((MEMBERS, COLS), f32),
            pltpu.VMEM((2 * MEMBERS, OBS), bf16),
            pltpu.VMEM((OBS, 3 * MEMBERS), bf16),
        ],
        compiler_params=params(60),
        cost_estimate=cost(8),
        name="drivers",
    )(here, order, count, weight, value, variance, index, chosen, wide, place, mine, other)


def update_kernel(chunk, late, apart, here_ref, count_ref, lhs_ref, driver_ref, centre_ref, inverse_ref, *refs):
    n_in = GROUPS if late else 1
    given, made = refs[:n_in], refs[-3 - (GROUPS if apart else 1) :]
    x, in_ref, out_ref = made[-3:]
    if late:
        for d in range(GROUPS):
            in_ref[lax.rem(here_ref[0] + GROUPS - d, GROUPS)] = given[d][...]
    else:
        in_ref = given[0]
    if not apart:
        out_ref = made[0]
    ins = [in_ref.at[q] for q in range(GROUPS)]
    outs = [out_ref.at[q] for q in range(GROUPS)]
    low = lax.broadcasted_iota(jnp.int32, (8, HALF), 0) < 4
    offsets = lax.broadcasted_iota(jnp.int32, (1, HALF), 1)
    first = here_ref[0] * CELLS + chunk * CHUNK

    def join(a, b):
        return jnp.where(low, a, pltpu.roll(b, 4, 0)), jnp.where(low, pltpu.roll(a, 4, 0), b)

    for p, ref in enumerate(ins):
        for h in range(2):
            x[h, 16 * p : 16 * p + 8] = ref[:, h * HALF : (h + 1) * HALF]
            x[h, 16 * p + 8 : 16 * p + 16] = ref[:, CHUNK + h * HALF : CHUNK + (h + 1) * HALF]
    for q in range(2):
        rest = join(ins[2 * q][:, 2 * CHUNK : PACKED], ins[2 * q + 1][:, 2 * CHUNK : PACKED])
        for h in range(2):
            x[h, 64 + 8 * q : 72 + 8 * q] = rest[h]

    def block(t, carry):
        count = count_ref[t]

        def apply(slots):
            width = 192 if slots == 64 else OBS
            height = MEMBERS if slots == 64 else 2 * MEMBERS
            lhs = lhs_ref[t, 0:slots]
            driver = driver_ref[t, 0:height, 0:width]
            for h in range(2):
                place = (first + h * HALF + offsets).astype(f32)
                x[h] = updated(x[h], place, lhs, driver, centre_ref[t, 0:slots], inverse_ref[t, 0:slots], slots)

        @pl.when((count > 0) & (count <= 64))
        def _():
            apply(64)

        @pl.when((count > 64) & (count <= 128))
        def _():
            apply(128)

        @pl.when(count > 128)
        def _():
            apply(OBS)

        return carry

    lax.fori_loop(0, BLOCKS, block, 0)
    for p, ref in enumerate(outs):
        for h in range(2):
            ref[:, h * HALF : (h + 1) * HALF] = x[h, 16 * p : 16 * p + 8]
            ref[:, CHUNK + h * HALF : CHUNK + (h + 1) * HALF] = x[h, 16 * p + 8 : 16 * p + 16]
    for q in range(2):
        a, b = join(x[0, 64 + 8 * q : 72 + 8 * q], x[1, 64 + 8 * q : 72 + 8 * q])
        outs[2 * q][:, 2 * CHUNK : PACKED] = a
        outs[2 * q + 1][:, 2 * CHUNK : PACKED] = b
    if apart:
        for d in range(GROUPS):
            made[d][...] = out_ref[lax.rem(here_ref[0] + d, GROUPS)]


def fixed(shape, index):
    return pl.BlockSpec(shape, lambda i: index, pipeline_mode=pl.Buffered(1))


def update(chunk, late, apart, index, here, terms, arrived, firsts):
    gathered = (GROUPS, 8, PACKED)
    shapes = [gathered[1:]] * GROUPS if apart else [gathered]
    return pl.pallas_call(
        functools.partial(update_kernel, chunk, late, apart),
        grid=(1,),
        out_shape=[jax.ShapeDtypeStruct(shape, f32) for shape in shapes],
        in_specs=smem(2)
        + [fixed(a.shape, (0, 0, 0)) for a in terms[1:]]
        + ([fixed((8, PACKED), (0, index))] * GROUPS if late else [fixed(gathered, (0, 0, index))])
        + [pl.BlockSpec(memory_space=pl.ANY)] * len(firsts),
        out_specs=[fixed(shape, (0,) * len(shape)) for shape in shapes],
        scratch_shapes=[pltpu.VMEM((2, MEMBERS, HALF), f32)] + [pltpu.VMEM(gathered, f32)] * 2,
        compiler_params=params(60),
        cost_estimate=cost(8),
        name="update",
    )(here, *terms, *arrived, *firsts)


def unpack_kernel(chunk, apart, rank_ref, *refs):
    out_ref, rows, sems = refs[-3:]
    copies = []
    for i in range(GROUPS):
        src = refs[i] if apart else refs[0].at[i]
        quarter = lax.rem(rank_ref[0] + GROUPS - i, GROUPS) if apart else i
        rows[i, 0:8, :] = src[:, 0:CHUNK]
        rows[i, 8:16, :] = src[:, CHUNK : 2 * CHUNK]
        rows[i, 16:20, 0:HALF] = src[0:4, 2 * CHUNK : PACKED]
        rows[i, 16:20, HALF:CHUNK] = src[4:8, 2 * CHUNK : PACKED]
        at = pl.multiple_of(quarter * CELLS + chunk * CHUNK, 128)
        copy = pltpu.make_async_copy(rows.at[i], out_ref.at[:, pl.ds(at, CHUNK)], sems.at[i])
        copy.start()
        copies.append(copy)
    for copy in copies:
        copy.wait()


def unpack(chunk, apart, rank, pieces, out):
    held = [] if out is None else [out]
    return pl.pallas_call(
        functools.partial(unpack_kernel, chunk, apart),
        out_shape=jax.ShapeDtypeStruct((ROWS, GROUPS * CELLS), f32),
        in_specs=smem(1) + whole(len(pieces)) + [pl.BlockSpec(memory_space=pl.ANY)] * len(held),
        out_specs=pl.BlockSpec(memory_space=pl.ANY),
        scratch_shapes=[pltpu.VMEM((GROUPS, ROWS, CHUNK), f32), pltpu.SemaphoreType.DMA((GROUPS,))],
        input_output_aliases={1 + len(pieces): 0} if held else {},
        compiler_params=params(60),
        cost_estimate=cost(2),
        name="unpack",
    )(rank, *pieces, *held)


def shifted(x, axis, size, by):
    return lax.ppermute(x, axis, [(i, (i + by) % size) for i in range(size)])


def exchanged(x):
    return lax.all_to_all(x, "member", split_axis=0, concat_axis=0, tiled=True)


def per_device(
    ensemble,
    block_order,
    obs_owner,
    interp_cells,
    interp_weight,
    obs_radius,
    obs_value,
    obs_variance,
):
    slabs = lax.axis_size("slab")
    member_rank = lax.axis_index("member")
    slab_rank = lax.axis_index("slab")
    rank = member_rank.reshape(1)
    slab = slab_rank.reshape(1)
    here = slab * GROUPS + rank

    cells = interp_cells.transpose(0, 2, 1)
    weight = interp_weight.transpose(0, 2, 1)
    early, *late, lists = pack(rank, slab, block_order, obs_owner, ensemble)
    entered = [exchanged(early)]
    keep, send = pick(slab, block_order, obs_owner, cells, lists, weight, ensemble, early)
    chip = keep + lax.ppermute(send, "slab", [(i, i ^ 1) for i in range(slabs)])
    near = [shifted(chip, "slab", slabs, by) for by in (2, -2)]
    far = [shifted(chip[:, :FAR], "slab", slabs, by) for by in (4, -4)]
    count, index, chosen, centre, inverse, wide, place = reach(
        here, block_order, obs_owner, cells, obs_radius, chip
    )
    summed = window(chip, near, far, [count])
    mine = lax.all_gather(summed, "member", axis=0, tiled=True)
    other = lax.ppermute(mine, "slab", [(i, i ^ 1) for i in range(slabs)])
    late = after(late, mine, entered[0][0, :, 0:128])
    late = [late[0]] + [shifted(late[d], "member", GROUPS, d) for d in range(1, GROUPS)]
    lhs, driver = drivers(
        here, block_order, count, weight, obs_value, obs_variance, index, chosen, wide, place, mine, other
    )
    terms = (count, lhs, driver, centre, inverse)

    made, firsts = [], []
    for c in range(CHUNKS):
        held = c in LATE
        at = LATE.index(c) if held else EARLY.index(c)
        made.append(update(c, held, c in PERMUTED, at, here, terms, late if held else entered, firsts))
        firsts = [made[c][0]]
    made[0] = after(made[0], *late[1:], made[1][0])
    made[2] = after(made[2], made[3][0])
    out = None
    for c, new in enumerate(made):
        if c in PERMUTED:
            back = [new[0]] + [shifted(new[d], "member", GROUPS, d) for d in range(1, GROUPS)]
        else:
            back = [exchanged(new[0])]
        out = unpack(c, c in PERMUTED, rank, back, out)
    return out


def solution(mesh):
    in_specs = (P("member", "slab"), P(), P(), P(), P(), P(), P(), P())
    out_specs = P("member", "slab")
    return jax.shard_map(
        per_device, mesh=mesh, in_specs=in_specs, out_specs=out_specs, check_vma=False
    )
```

```python
import functools

import jax
import jax.numpy as jnp
from jax import lax
from jax.experimental import pallas as pl
from jax.experimental.pallas import tpu as pltpu
from jax.sharding import PartitionSpec as P

MEMBERS = 80
BLOCKS = 4
POINTS = 4
OBS = 256
GROUPS = 4
ROWS = MEMBERS // GROUPS
PADDED = 24
CELLS = 12288
CHUNKS = 6
EARLY = (0, 1, 2, 3)
LATE = (4, 5)
EXITS = ((0, 1), (2, 3), (4, 5))
CHUNK = CELLS // CHUNKS
HALF = CHUNK // 2
PACKED = 5 * HALF
COLS = OBS + (BLOCKS - 1) * POINTS * OBS
PART = COLS // 2
FAR = 128 + POINTS * 128
WIDE = 1024
UNROLL = 4
MIB = 1024 * 1024

f32 = jnp.float32
bf16 = jnp.bfloat16


def split(x):
    hi = x.astype(bf16)
    lo = (x - hi.astype(f32)).astype(bf16)
    return hi, lo


def whole(n):
    return [pl.BlockSpec(memory_space=pltpu.VMEM)] * n


def smem(n):
    return [pl.BlockSpec(memory_space=pltpu.SMEM)] * n


def params(mib):
    return pltpu.CompilerParams(vmem_limit_bytes=mib * MIB)


def cost(micros):
    return pl.CostEstimate(flops=0, bytes_accessed=int(micros * 1024), transcendentals=0)


def place_piece(out, o, ens_ref, c):
    at, mid = c * CHUNK, c * CHUNK + HALF
    out[:, o : o + CHUNK] = ens_ref[0:8, at : at + CHUNK]
    out[:, o + CHUNK : o + 2 * CHUNK] = ens_ref[8:16, at : at + CHUNK]
    out[0:4, o + 2 * CHUNK : o + PACKED] = ens_ref[16:20, at : at + HALF]
    out[4:8, o + 2 * CHUNK : o + PACKED] = ens_ref[16:20, mid : mid + HALF]


def pack_kernel(rank_ref, slab_ref, order_ref, owner_ref, ens_ref, early_ref, *refs):
    late_refs, lists_ref, owners = refs[:GROUPS], refs[GROUPS], refs[GROUPS + 1]
    step = pl.program_id(0)

    @pl.when(step == 1)
    def _():
        owners[...] = jnp.full_like(owners, -1)
        for t in range(BLOCKS):
            owners[t : t + 1, :] = owner_ref[pl.ds(order_ref[t], 1), :]
        row = lax.broadcasted_iota(jnp.int32, (OBS, OBS), 0)
        column = lax.broadcasted_iota(jnp.int32, (OBS, OBS), 1)
        before = jnp.where(row < column, f32(1.0), f32(0.0)).astype(bf16)
        inside = (owners[...] >> 2) == slab_ref[0]
        ahead = jnp.dot(jnp.where(inside, f32(1.0), f32(0.0)).astype(bf16), before, preferred_element_type=f32)
        index = jnp.where(inside, ahead, f32(-1.0)).T
        for t in range(BLOCKS):
            hit = index[:, t : t + 1] == column.astype(f32)
            held = jnp.sum(jnp.where(hit, row.astype(f32), f32(0.0)), axis=0, keepdims=True)
            lists_ref[t : t + 1, :] = held.astype(jnp.int32)
        total = jnp.sum(jnp.where(inside, f32(1.0), f32(0.0)), axis=1, keepdims=True)
        lists_ref[BLOCKS : 2 * BLOCKS, :] = jnp.broadcast_to(total[0:BLOCKS], (BLOCKS, OBS)).astype(jnp.int32)

    for i, c in enumerate(EARLY):
        place_piece(early_ref.at[0], i * PACKED, ens_ref, c)
    for d in range(GROUPS):

        @pl.when(step == d)
        def _():
            for i, c in enumerate(LATE):
                place_piece(late_refs[d], i * PACKED, ens_ref, c)


def pack(rank, slab, order, owner, ensemble):
    late = jax.ShapeDtypeStruct((8, PACKED * len(LATE)), f32)

    def quarter(i, rank_ref):
        return lax.rem(rank_ref[0] + i, GROUPS)

    return pl.pallas_call(
        pack_kernel,
        grid_spec=pltpu.PrefetchScalarGridSpec(
            num_scalar_prefetch=3,
            grid=(GROUPS,),
            in_specs=[
                pl.BlockSpec((BLOCKS, OBS), lambda i, *_: (0, 0)),
                pl.BlockSpec((ROWS, CELLS), lambda i, r, *_: (0, quarter(i, r))),
            ],
            out_specs=[pl.BlockSpec((1, 8, PACKED * len(EARLY)), lambda i, r, *_: (quarter(i, r), 0, 0))]
            + [pl.BlockSpec(late.shape, lambda i, *_: (0, 0))] * GROUPS
            + [pl.BlockSpec((2 * BLOCKS, OBS), lambda i, *_: (0, 0))],
            scratch_shapes=[pltpu.VMEM((2 * BLOCKS, OBS), jnp.int32)],
        ),
        out_shape=[jax.ShapeDtypeStruct((GROUPS, 8, PACKED * len(EARLY)), f32)]
        + [late] * GROUPS
        + [jax.ShapeDtypeStruct((2 * BLOCKS, OBS), jnp.int32)],
        compiler_params=params(60),
        cost_estimate=cost(3),
        name="pack",
    )(rank, slab, order, owner, ensemble)


def after_kernel(*refs):
    pass


def after(xs, *firsts):
    anywhere = pl.BlockSpec(memory_space=pl.ANY)
    n = len(xs)
    return pl.pallas_call(
        after_kernel,
        out_shape=[jax.ShapeDtypeStruct(x.shape, x.dtype) for x in xs],
        in_specs=[anywhere] * (n + len(firsts)),
        out_specs=[anywhere] * n,
        input_output_aliases={i: i for i in range(n)},
        compiler_params=params(60),
        cost_estimate=cost(1),
        name="after",
    )(*xs, *firsts)


def pick_kernel(slab_ref, order_ref, owner_ref, cells_ref, held, weight_ref, ens_ref, after_ref, keep_ref, send_ref, *bufs):
    del after_ref
    slab = slab_ref[0]
    buf = bufs[POINTS]
    for point in bufs[:POINTS]:
        point[...] = jnp.zeros_like(point)

    blocks = [order_ref[t] for t in range(BLOCKS)]
    lanes = lax.broadcasted_iota(jnp.int32, (8, 128), 1)
    lanes4 = lax.broadcasted_iota(jnp.int32, (4, 128), 1)
    for t in range(BLOCKS):
        count = held[BLOCKS + t, 0]
        b = blocks[t]

        def some(s, carry):
            for u in range(UNROLL):
                i = s * UNROLL + u
                valid = i < count
                j = jnp.where(valid, held[t, i], 0)
                base = (owner_ref[b, j] & 3) * CELLS
                n = j & 127
                lane = jnp.where(valid, n, -1)
                hit = lanes == lane
                hit4 = lanes4 == lane
                dst = pl.ds(pl.multiple_of(t * OBS + (j - n), 128), 128)
                for k in range(POINTS):
                    point = bufs[k].at[u]
                    place = jnp.where(valid, base + cells_ref[b, k, j], 0)
                    src = pl.ds(pl.multiple_of((place >> 7) * 128, 128), 128)
                    shift = (n - place) & 127
                    point[0:8, dst] = jnp.where(hit, pltpu.roll(ens_ref[0:8, src], shift, 1), point[0:8, dst])
                    point[8:16, dst] = jnp.where(hit, pltpu.roll(ens_ref[8:16, src], shift, 1), point[8:16, dst])
                    point[16:20, dst] = jnp.where(hit4, pltpu.roll(ens_ref[16:20, src], shift, 1), point[16:20, dst])
            return carry

        lax.fori_loop(0, (count + UNROLL - 1) // UNROLL, some, 0)
    points = [sum(point[u] for u in range(1, UNROLL)) + point[0] for point in bufs[:POINTS]]
    weight = weight_ref[blocks[0]]
    total = points[0][:, 0:OBS] * weight[0:1, :]
    for k in range(1, POINTS):
        total = total + points[k][:, 0:OBS] * weight[k : k + 1, :]
    for h in range(2):
        half = slice(h * 128, h * 128 + 128)
        buf[h, :, 0:128] = total[:, half]
        for t in range(1, BLOCKS):
            for k in range(POINTS):
                o = 128 + ((t - 1) * POINTS + k) * 128
                at = t * OBS + h * 128
                buf[h, :, o : o + 128] = points[k][:, at : at + 128]
    part = lax.rem(slab, 2)
    keep_ref[...] = buf[part]
    send_ref[...] = buf[1 - part]


def pick(slab, order, owner, cells, lists, weight, ensemble, after):
    return pl.pallas_call(
        pick_kernel,
        out_shape=[jax.ShapeDtypeStruct((PADDED, PART), f32)] * 2,
        in_specs=smem(5) + whole(2) + [pl.BlockSpec(memory_space=pl.ANY)],
        out_specs=whole(2),
        scratch_shapes=[pltpu.VMEM((UNROLL, PADDED, BLOCKS * OBS), f32)] * POINTS
        + [pltpu.VMEM((2, PADDED, PART), f32)],
        compiler_params=params(60),
        cost_estimate=cost(8),
        name="pick",
    )(slab, order, owner, cells, lists, weight, ensemble, after)


def window_kernel(chip_ref, *refs):
    near, far, out_ref = refs[0:2], refs[2:4], refs[-1]
    total = chip_ref[...] + near[0][...] + near[1][...]
    out_ref[:, 0:FAR] = total[:, 0:FAR] + far[0][...] + far[1][...]
    out_ref[:, FAR:PART] = total[:, FAR:PART]


def window(chip, near, far, firsts):
    return pl.pallas_call(
        window_kernel,
        out_shape=jax.ShapeDtypeStruct((PADDED, PART), f32),
        in_specs=whole(5) + [pl.BlockSpec(memory_space=pl.ANY)] * len(firsts),
        out_specs=pl.BlockSpec(memory_space=pltpu.VMEM),
        compiler_params=params(4),
        cost_estimate=cost(1),
        name="window",
    )(chip, *near, *far, *firsts)


def reach_kernel(here_ref, order_ref, owner_ref, cells_ref, radius_ref, after_ref, *refs):
    del after_ref
    count_ref, index_ref, chosen_ref, centre_ref, inverse_ref, wide_ref, place = refs
    slot = lax.broadcasted_iota(jnp.int32, (OBS, OBS), 0)
    column = lax.broadcasted_iota(jnp.int32, (OBS, OBS), 1)
    before = jnp.where(slot < column, f32(1.0), f32(0.0)).astype(bf16)
    begin = (here_ref[0] * CELLS).astype(f32)
    end = begin + f32(CELLS - 1)
    place[:, 0:OBS] = jnp.zeros((1, OBS), f32)
    for t in range(BLOCKS):
        b = order_ref[t]
        everywhere = (owner_ref[pl.ds(b, 1), :] * CELLS + cells_ref[b]).astype(f32)
        if t > 0:
            for k in range(POINTS):
                o = OBS + (t - 1) * POINTS * OBS + k * OBS
                place[:, o : o + OBS] = everywhere[k : k + 1, :]
        centre = everywhere[0:1, :]
        radius = radius_ref[pl.ds(b, 1), :].astype(f32)
        inverse = f32(1.0) / radius
        terms = jnp.concatenate([centre, inverse, jnp.zeros((6, OBS), f32)], axis=0).T
        wide_ref[t, 0] = jnp.broadcast_to(terms[:, 0:1], (OBS, 128))
        wide_ref[t, 1] = jnp.broadcast_to(terms[:, 1:2], (OBS, 128))
        away = jnp.maximum(jnp.maximum(begin - centre, centre - end), f32(0.0))
        active = jnp.where(away < radius, f32(1.0), f32(0.0))
        count_ref[t] = jnp.sum(active).astype(jnp.int32)
        ahead = jnp.dot(jnp.broadcast_to(active, (8, OBS)).astype(bf16), before, preferred_element_type=f32)
        index = jnp.where(active > 0, ahead[0:1, :], f32(-1.0)).astype(jnp.int32)
        index_ref[t] = index
        hit = index == slot
        chosen_ref[t] = jnp.where(hit, f32(1.0), f32(0.0)).astype(bf16)
        centre_ref[t] = jnp.broadcast_to(jnp.sum(jnp.where(hit, centre, f32(0.0)), axis=1, keepdims=True), (OBS, 128))
        inverse_ref[t] = jnp.broadcast_to(jnp.sum(jnp.where(hit, inverse, f32(0.0)), axis=1, keepdims=True), (OBS, 128))


def reach(here, order, owner, cells, radius, first):
    shape = jax.ShapeDtypeStruct
    return pl.pallas_call(
        reach_kernel,
        out_shape=[
            shape((BLOCKS,), jnp.int32),
            shape((BLOCKS, 1, OBS), jnp.int32),
            shape((BLOCKS, OBS, OBS), bf16),
            shape((BLOCKS, OBS, 128), f32),
            shape((BLOCKS, OBS, 128), f32),
            shape((BLOCKS, 2, OBS, 128), f32),
            shape((1, COLS), f32),
        ],
        in_specs=smem(2) + whole(3) + [pl.BlockSpec(memory_space=pl.ANY)],
        out_specs=smem(1) + whole(6),
        compiler_params=params(60),
        cost_estimate=cost(2),
        name="reach",
    )(here, order, owner, cells, radius, first)


def updated(x, place, lhs, driver, centre, inverse, slots):
    reps = x.shape[1] // 128
    mean = jnp.sum(x, axis=0, keepdims=True) * f32(1.0 / MEMBERS)
    hi, lo = split(x - mean)
    cov = jnp.dot(lhs, jnp.concatenate([hi, lo, hi], axis=0), preferred_element_type=f32)
    centre = jnp.concatenate([centre] * reps, axis=1)
    inverse = jnp.concatenate([inverse] * reps, axis=1)
    loc = jnp.maximum(f32(0.0), f32(1.0) - jnp.abs(place - centre) * inverse)
    hi, lo = split(loc * cov)
    if slots == 64:
        return x + jnp.dot(driver, jnp.concatenate([hi, lo, hi], axis=0), preferred_element_type=f32)
    if slots == 128:
        both = jnp.dot(driver, jnp.concatenate([hi, lo], axis=0), preferred_element_type=f32)
        return x + (both[:MEMBERS] + both[MEMBERS:])
    both = jnp.dot(driver, hi, preferred_element_type=f32)
    rest = jnp.dot(driver[:MEMBERS], lo, preferred_element_type=f32)
    return x + (both[:MEMBERS] + both[MEMBERS:] + rest)


def drivers_kernel(here_ref, order_ref, count_ref, *refs):
    weight_ref, value_ref, variance_ref, index_ref, chosen_ref, wide, place, mine_ref, other_ref = refs[:9]
    lhs_ref, driver_ref, z, full, whole_lhs = refs[9:]
    part = lax.rem(here_ref[0] // GROUPS, 2)
    for src, h in ((mine_ref, part), (other_ref, 1 - part)):
        for p in range(GROUPS):
            for i in range(PART // 128):
                cols = slice(i * 128, i * 128 + 128)
                at = pl.ds(pl.multiple_of(i * OBS + h * 128, 128), 128)
                z[16 * p : 16 * p + 16, at] = src[PADDED * p : PADDED * p + 16, cols]
                z[64 + 4 * p : 68 + 4 * p, at] = src[PADDED * p + 16 : PADDED * p + 20, cols]

    for t in range(BLOCKS):
        b = order_ref[t]
        start = OBS + (t - 1) * POINTS * OBS
        weight = weight_ref[b]
        if t == 0:
            prior = z[:, 0:OBS]
        else:
            prior = z[:, start : start + OBS] * weight[0:1, :]
            for k in range(1, POINTS):
                prior = prior + z[:, start + k * OBS : start + (k + 1) * OBS] * weight[k : k + 1, :]
        value = value_ref[pl.ds(b, 1), :]
        variance = variance_ref[pl.ds(b, 1), :]
        ybar = jnp.sum(prior, axis=0, keepdims=True) * f32(1.0 / MEMBERS)
        anomaly = prior - ybar
        spread = jnp.sum(anomaly * anomaly, axis=0, keepdims=True) * f32(1.0 / (MEMBERS - 1))
        gain = f32(1.0) / (spread + variance)
        shrink = -gain / (f32(1.0) + jnp.sqrt(variance * gain))
        coeff = gain * (value - ybar)
        driver = coeff + shrink * anomaly
        hi, lo = split((anomaly * f32(1.0 / (MEMBERS - 1))).T)
        lhs = jnp.concatenate([hi, hi, lo], axis=1)
        dhi, dlo = split(driver)
        both = jnp.concatenate([dhi, dlo], axis=0)

        if t < BLOCKS - 1:
            whole_lhs[...] = lhs
            full[...] = both

            def evolve(i, carry):
                cols = pl.ds(pl.multiple_of(OBS + i * WIDE, 128), WIDE)
                z[:, cols] = updated(z[:, cols], place[:, cols], whole_lhs[...], full[...], wide[t, 0], wide[t, 1], OBS)
                return carry

            lax.fori_loop(t * POINTS * OBS // WIDE, (BLOCKS - 1) * POINTS * OBS // WIDE, evolve, 0)

        count = count_ref[t]
        lhs_ref[t] = jnp.dot(chosen_ref[t], lhs, preferred_element_type=f32).astype(bf16)
        nt = (((1,), (1,)), ((), ()))

        @pl.when(count <= 64)
        def _():
            slot = lax.broadcasted_iota(jnp.int32, (OBS, OBS), 0)
            again = jnp.where(index_ref[t] == (slot & 63), f32(1.0), f32(0.0)).astype(bf16)
            kept = lax.dot_general(both, again, nt, preferred_element_type=f32)
            lane = lax.broadcasted_iota(jnp.int32, (MEMBERS, OBS), 1)
            driver_ref[t, 0:MEMBERS] = jnp.where(lane < 128, kept[:MEMBERS], kept[MEMBERS:]).astype(bf16)

        @pl.when(count > 64)
        def _():
            kept = lax.dot_general(both, chosen_ref[t], nt, preferred_element_type=f32).astype(bf16)
            driver_ref[t] = kept

            @pl.when(count <= 128)
            def _():
                driver_ref[t, 0:MEMBERS, 128:256] = kept[:MEMBERS, 0:128]
                driver_ref[t, MEMBERS : 2 * MEMBERS, 128:256] = jnp.zeros((MEMBERS, 128), bf16)


def drivers(here, order, count, weight, value, variance, index, chosen, wide, place, mine, other):
    return pl.pallas_call(
        drivers_kernel,
        out_shape=[
            jax.ShapeDtypeStruct((BLOCKS, OBS, 3 * MEMBERS), bf16),
            jax.ShapeDtypeStruct((BLOCKS, 2 * MEMBERS, OBS), bf16),
        ],
        in_specs=smem(3) + whole(9),
        out_specs=whole(2),
        scratch_shapes=[
            pltpu.VMEM((MEMBERS, COLS), f32),
            pltpu.VMEM((2 * MEMBERS, OBS), bf16),
            pltpu.VMEM((OBS, 3 * MEMBERS), bf16),
        ],
        compiler_params=params(60),
        cost_estimate=cost(8),
        name="drivers",
    )(here, order, count, weight, value, variance, index, chosen, wide, place, mine, other)


def update_kernel(chunk, late, apart, here_ref, count_ref, lhs_ref, driver_ref, centre_ref, inverse_ref, *refs):
    n_in = GROUPS if late else 1
    given, made = refs[:n_in], refs[-3 - (GROUPS if apart else 1) :]
    x, in_ref, out_ref = made[-3:]
    if late:
        for d in range(GROUPS):
            in_ref[lax.rem(here_ref[0] + GROUPS - d, GROUPS)] = given[d][...]
    else:
        in_ref = given[0]
    if not apart:
        out_ref = made[0]
    ins = [in_ref.at[q] for q in range(GROUPS)]
    outs = [out_ref.at[q] for q in range(GROUPS)]
    low = lax.broadcasted_iota(jnp.int32, (8, HALF), 0) < 4
    offsets = lax.broadcasted_iota(jnp.int32, (1, HALF), 1)
    first = here_ref[0] * CELLS + (chunk + pl.program_id(0)) * CHUNK

    def join(a, b):
        return jnp.where(low, a, pltpu.roll(b, 4, 0)), jnp.where(low, pltpu.roll(a, 4, 0), b)

    for p, ref in enumerate(ins):
        for h in range(2):
            x[h, 16 * p : 16 * p + 8] = ref[:, h * HALF : (h + 1) * HALF]
            x[h, 16 * p + 8 : 16 * p + 16] = ref[:, CHUNK + h * HALF : CHUNK + (h + 1) * HALF]
    for q in range(2):
        rest = join(ins[2 * q][:, 2 * CHUNK : PACKED], ins[2 * q + 1][:, 2 * CHUNK : PACKED])
        for h in range(2):
            x[h, 64 + 8 * q : 72 + 8 * q] = rest[h]

    def block(t, carry):
        count = count_ref[t]

        def apply(slots):
            width = 192 if slots == 64 else OBS
            height = MEMBERS if slots == 64 else 2 * MEMBERS
            lhs = lhs_ref[t, 0:slots]
            driver = driver_ref[t, 0:height, 0:width]
            for h in range(2):
                place = (first + h * HALF + offsets).astype(f32)
                x[h] = updated(x[h], place, lhs, driver, centre_ref[t, 0:slots], inverse_ref[t, 0:slots], slots)

        @pl.when((count > 0) & (count <= 64))
        def _():
            apply(64)

        @pl.when((count > 64) & (count <= 128))
        def _():
            apply(128)

        @pl.when(count > 128)
        def _():
            apply(OBS)

        return carry

    lax.fori_loop(0, BLOCKS, block, 0)
    for p, ref in enumerate(outs):
        for h in range(2):
            ref[:, h * HALF : (h + 1) * HALF] = x[h, 16 * p : 16 * p + 8]
            ref[:, CHUNK + h * HALF : CHUNK + (h + 1) * HALF] = x[h, 16 * p + 8 : 16 * p + 16]
    for q in range(2):
        a, b = join(x[0, 64 + 8 * q : 72 + 8 * q], x[1, 64 + 8 * q : 72 + 8 * q])
        outs[2 * q][:, 2 * CHUNK : PACKED] = a
        outs[2 * q + 1][:, 2 * CHUNK : PACKED] = b
    if apart:
        for d in range(GROUPS):
            made[d][...] = out_ref[lax.rem(here_ref[0] + d, GROUPS)]


def fixed(shape, index):
    return pl.BlockSpec(shape, lambda i: index, pipeline_mode=pl.Buffered(1))


def update(chunks, late, apart, index, here, terms, arrived, firsts):
    gathered = (GROUPS, 8, PACKED)
    shapes = [gathered[1:]] * GROUPS if apart else [gathered]
    n = len(chunks)

    def wide(shape):
        return jax.ShapeDtypeStruct(shape[:-1] + (PACKED * n,), f32)

    def blocks(shape, at):
        return pl.BlockSpec(shape, lambda i: (0,) * (len(shape) - 1) + (at + i,))

    return pl.pallas_call(
        functools.partial(update_kernel, chunks[0], late, apart),
        grid=(n,),
        out_shape=[wide(shape) for shape in shapes],
        in_specs=smem(2)
        + [fixed(a.shape, (0, 0, 0)) for a in terms[1:]]
        + ([blocks(gathered[1:], index)] * GROUPS if late else [blocks(gathered, index)])
        + [pl.BlockSpec(memory_space=pl.ANY)] * len(firsts),
        out_specs=[blocks(shape, 0) for shape in shapes],
        scratch_shapes=[pltpu.VMEM((2, MEMBERS, HALF), f32)] + [pltpu.VMEM(gathered, f32)] * 2,
        compiler_params=params(60),
        cost_estimate=cost(8),
        name="update",
    )(here, *terms, *arrived, *firsts)


def unpack_kernel(chunk, apart, rank_ref, *refs):
    out_ref, rows, sems = refs[-3:]
    copies = []
    for i in range(GROUPS):
        src = refs[i] if apart else refs[0].at[i]
        quarter = lax.rem(rank_ref[0] + GROUPS - i, GROUPS) if apart else i
        rows[i, 0:8, :] = src[:, 0:CHUNK]
        rows[i, 8:16, :] = src[:, CHUNK : 2 * CHUNK]
        rows[i, 16:20, 0:HALF] = src[0:4, 2 * CHUNK : PACKED]
        rows[i, 16:20, HALF:CHUNK] = src[4:8, 2 * CHUNK : PACKED]
        at = pl.multiple_of(quarter * CELLS + (chunk + pl.program_id(0)) * CHUNK, 128)
        copy = pltpu.make_async_copy(rows.at[i], out_ref.at[:, pl.ds(at, CHUNK)], sems.at[i])
        copy.start()
        copies.append(copy)
    for copy in copies:
        copy.wait()


def unpack(chunks, apart, rank, pieces, out):
    held = [] if out is None else [out]
    shape = (8, PACKED) if apart else (GROUPS, 8, PACKED)
    block = pl.BlockSpec(shape, lambda i: (0,) * (len(shape) - 1) + (i,))
    return pl.pallas_call(
        functools.partial(unpack_kernel, chunks[0], apart),
        grid=(len(chunks),),
        out_shape=jax.ShapeDtypeStruct((ROWS, GROUPS * CELLS), f32),
        in_specs=smem(1) + [block] * len(pieces) + [pl.BlockSpec(memory_space=pl.ANY)] * len(held),
        out_specs=pl.BlockSpec(memory_space=pl.ANY),
        scratch_shapes=[pltpu.VMEM((GROUPS, ROWS, CHUNK), f32), pltpu.SemaphoreType.DMA((GROUPS,))],
        input_output_aliases={1 + len(pieces): 0} if held else {},
        compiler_params=params(60),
        cost_estimate=cost(2),
        name="unpack",
    )(rank, *pieces, *held)


def shifted(x, axis, size, by):
    return lax.ppermute(x, axis, [(i, (i + by) % size) for i in range(size)])


def exchanged(x):
    return lax.all_to_all(x, "member", split_axis=0, concat_axis=0, tiled=True)


def per_device(
    ensemble,
    block_order,
    obs_owner,
    interp_cells,
    interp_weight,
    obs_radius,
    obs_value,
    obs_variance,
):
    slabs = lax.axis_size("slab")
    member_rank = lax.axis_index("member")
    slab_rank = lax.axis_index("slab")
    rank = member_rank.reshape(1)
    slab = slab_rank.reshape(1)
    here = slab * GROUPS + rank

    cells = interp_cells.transpose(0, 2, 1)
    weight = interp_weight.transpose(0, 2, 1)
    early, *late, lists = pack(rank, slab, block_order, obs_owner, ensemble)
    entered = [exchanged(early)]
    keep, send = pick(slab, block_order, obs_owner, cells, lists, weight, ensemble, early)
    chip = keep + lax.ppermute(send, "slab", [(i, i ^ 1) for i in range(slabs)])
    near = [shifted(chip, "slab", slabs, by) for by in (2, -2)]
    far = [shifted(chip[:, :FAR], "slab", slabs, by) for by in (4, -4)]
    count, index, chosen, centre, inverse, wide, place = reach(
        here, block_order, obs_owner, cells, obs_radius, chip
    )
    summed = window(chip, near, far, [count])
    mine = lax.all_gather(summed, "member", axis=0, tiled=True)
    other = lax.ppermute(mine, "slab", [(i, i ^ 1) for i in range(slabs)])
    late = after(late, mine, entered[0][0, :, 0:128])
    late = [late[0]] + [shifted(late[d], "member", GROUPS, d) for d in range(1, GROUPS)]
    lhs, driver = drivers(
        here, block_order, count, weight, obs_value, obs_variance, index, chosen, wide, place, mine, other
    )
    terms = (count, lhs, driver, centre, inverse)

    made, firsts = [], []
    for e, chunks in enumerate(EXITS):
        held = chunks[0] in LATE
        group = LATE if held else EARLY
        at = group.index(chunks[0])
        new = update(chunks, held, e > 0, at, here, terms, late if held else entered, firsts)
        if e == 0:
            new = after(new, *late[1:])
        made.append(new)
        firsts = [new[0]]
    out = None
    for e, (chunks, new) in enumerate(zip(EXITS, made)):
        if e == 0:
            back = [exchanged(new[0])]
        else:
            back = [new[0]] + [shifted(new[d], "member", GROUPS, d) for d in range(1, GROUPS)]
        out = unpack(chunks, e > 0, rank, back, out)
    return out


def solution(mesh):
    in_specs = (P("member", "slab"), P(), P(), P(), P(), P(), P(), P())
    out_specs = P("member", "slab")
    return jax.shard_map(
        per_device, mesh=mesh, in_specs=in_specs, out_specs=out_specs, check_vma=False
    )
```

```python
import functools

import jax
import jax.numpy as jnp
from jax import lax
from jax.experimental import pallas as pl
from jax.experimental.pallas import tpu as pltpu
from jax.sharding import PartitionSpec as P

MEMBERS = 80
BLOCKS = 4
POINTS = 4
OBS = 256
GROUPS = 4
ROWS = MEMBERS // GROUPS
PADDED = 24
CELLS = 12288
CHUNKS = 6
EARLY = (0, 1, 2, 3)
LATE = (4, 5)
EXITS = ((0, 1), (2, 3), (4, 5))
CHUNK = CELLS // CHUNKS
HALF = CHUNK // 2
PACKED = 5 * HALF
COLS = OBS + (BLOCKS - 1) * POINTS * OBS
PART = COLS // 2
FAR = 128 + POINTS * 128
WIDE = 1024
UNROLL = 4
MIB = 1024 * 1024

f32 = jnp.float32
bf16 = jnp.bfloat16


def split(x):
    hi = x.astype(bf16)
    lo = (x - hi.astype(f32)).astype(bf16)
    return hi, lo


def whole(n):
    return [pl.BlockSpec(memory_space=pltpu.VMEM)] * n


def smem(n):
    return [pl.BlockSpec(memory_space=pltpu.SMEM)] * n


def params(mib):
    return pltpu.CompilerParams(vmem_limit_bytes=mib * MIB)


def cost(micros):
    return pl.CostEstimate(flops=0, bytes_accessed=int(micros * 1024), transcendentals=0)


def place_piece(out, o, ens_ref, c):
    at, mid = c * CHUNK, c * CHUNK + HALF
    out[:, o : o + CHUNK] = ens_ref[0:8, at : at + CHUNK]
    out[:, o + CHUNK : o + 2 * CHUNK] = ens_ref[8:16, at : at + CHUNK]
    out[0:4, o + 2 * CHUNK : o + PACKED] = ens_ref[16:20, at : at + HALF]
    out[4:8, o + 2 * CHUNK : o + PACKED] = ens_ref[16:20, mid : mid + HALF]


def pack_kernel(rank_ref, slab_ref, order_ref, owner_ref, ens_ref, early_ref, *refs):
    late_refs, lists_ref, owners = refs[:GROUPS], refs[GROUPS], refs[GROUPS + 1]
    step = pl.program_id(0)

    @pl.when(step == 1)
    def _():
        owners[...] = jnp.full_like(owners, -1)
        for t in range(BLOCKS):
            owners[t : t + 1, :] = owner_ref[pl.ds(order_ref[t], 1), :]
        row = lax.broadcasted_iota(jnp.int32, (OBS, OBS), 0)
        column = lax.broadcasted_iota(jnp.int32, (OBS, OBS), 1)
        before = jnp.where(row < column, f32(1.0), f32(0.0)).astype(bf16)
        inside = (owners[...] >> 2) == slab_ref[0]
        ahead = jnp.dot(jnp.where(inside, f32(1.0), f32(0.0)).astype(bf16), before, preferred_element_type=f32)
        index = jnp.where(inside, ahead, f32(-1.0)).T
        for t in range(BLOCKS):
            hit = index[:, t : t + 1] == column.astype(f32)
            held = jnp.sum(jnp.where(hit, row.astype(f32), f32(0.0)), axis=0, keepdims=True)
            lists_ref[t : t + 1, :] = held.astype(jnp.int32)
        total = jnp.sum(jnp.where(inside, f32(1.0), f32(0.0)), axis=1, keepdims=True)
        lists_ref[BLOCKS : 2 * BLOCKS, :] = jnp.broadcast_to(total[0:BLOCKS], (BLOCKS, OBS)).astype(jnp.int32)

    for i, c in enumerate(EARLY):
        place_piece(early_ref.at[0], i * PACKED, ens_ref, c)
    for d in range(GROUPS):

        @pl.when(step == d)
        def _():
            for i, c in enumerate(LATE):
                place_piece(late_refs[d], i * PACKED, ens_ref, c)


def pack(rank, slab, order, owner, ensemble):
    late = jax.ShapeDtypeStruct((8, PACKED * len(LATE)), f32)

    def quarter(i, rank_ref):
        return lax.rem(rank_ref[0] + i, GROUPS)

    return pl.pallas_call(
        pack_kernel,
        grid_spec=pltpu.PrefetchScalarGridSpec(
            num_scalar_prefetch=3,
            grid=(GROUPS,),
            in_specs=[
                pl.BlockSpec((BLOCKS, OBS), lambda i, *_: (0, 0)),
                pl.BlockSpec((ROWS, CELLS), lambda i, r, *_: (0, quarter(i, r))),
            ],
            out_specs=[pl.BlockSpec((1, 8, PACKED * len(EARLY)), lambda i, r, *_: (quarter(i, r), 0, 0))]
            + [pl.BlockSpec(late.shape, lambda i, *_: (0, 0))] * GROUPS
            + [pl.BlockSpec((2 * BLOCKS, OBS), lambda i, *_: (0, 0))],
            scratch_shapes=[pltpu.VMEM((2 * BLOCKS, OBS), jnp.int32)],
        ),
        out_shape=[jax.ShapeDtypeStruct((GROUPS, 8, PACKED * len(EARLY)), f32)]
        + [late] * GROUPS
        + [jax.ShapeDtypeStruct((2 * BLOCKS, OBS), jnp.int32)],
        compiler_params=params(60),
        cost_estimate=cost(3),
        name="pack",
    )(rank, slab, order, owner, ensemble)


def after_kernel(*refs):
    pass


def after(xs, *firsts):
    anywhere = pl.BlockSpec(memory_space=pl.ANY)
    n = len(xs)
    return pl.pallas_call(
        after_kernel,
        out_shape=[jax.ShapeDtypeStruct(x.shape, x.dtype) for x in xs],
        in_specs=[anywhere] * (n + len(firsts)),
        out_specs=[anywhere] * n,
        input_output_aliases={i: i for i in range(n)},
        compiler_params=params(60),
        cost_estimate=cost(1),
        name="after",
    )(*xs, *firsts)


def pick_kernel(slab_ref, order_ref, owner_ref, cells_ref, held, weight_ref, ens_ref, after_ref, keep_ref, send_ref, *bufs):
    del after_ref
    slab = slab_ref[0]
    buf = bufs[POINTS]
    for point in bufs[:POINTS]:
        point[...] = jnp.zeros_like(point)

    blocks = [order_ref[t] for t in range(BLOCKS)]
    lanes = lax.broadcasted_iota(jnp.int32, (8, 128), 1)
    lanes4 = lax.broadcasted_iota(jnp.int32, (4, 128), 1)
    for t in range(BLOCKS):
        count = held[BLOCKS + t, 0]
        b = blocks[t]

        def some(s, carry):
            for u in range(UNROLL):
                i = s * UNROLL + u
                valid = i < count
                j = jnp.where(valid, held[t, i], 0)
                base = (owner_ref[b, j] & 3) * CELLS
                n = j & 127
                lane = jnp.where(valid, n, -1)
                hit = lanes == lane
                hit4 = lanes4 == lane
                dst = pl.ds(pl.multiple_of(t * OBS + (j - n), 128), 128)
                for k in range(POINTS):
                    point = bufs[k].at[u]
                    place = jnp.where(valid, base + cells_ref[b, k, j], 0)
                    src = pl.ds(pl.multiple_of((place >> 7) * 128, 128), 128)
                    shift = (n - place) & 127
                    point[0:8, dst] = jnp.where(hit, pltpu.roll(ens_ref[0:8, src], shift, 1), point[0:8, dst])
                    point[8:16, dst] = jnp.where(hit, pltpu.roll(ens_ref[8:16, src], shift, 1), point[8:16, dst])
                    point[16:20, dst] = jnp.where(hit4, pltpu.roll(ens_ref[16:20, src], shift, 1), point[16:20, dst])
            return carry

        lax.fori_loop(0, (count + UNROLL - 1) // UNROLL, some, 0)
    points = [sum(point[u] for u in range(1, UNROLL)) + point[0] for point in bufs[:POINTS]]
    weight = weight_ref[blocks[0]]
    total = points[0][:, 0:OBS] * weight[0:1, :]
    for k in range(1, POINTS):
        total = total + points[k][:, 0:OBS] * weight[k : k + 1, :]
    for h in range(2):
        half = slice(h * 128, h * 128 + 128)
        buf[h, :, 0:128] = total[:, half]
        for t in range(1, BLOCKS):
            for k in range(POINTS):
                o = 128 + ((t - 1) * POINTS + k) * 128
                at = t * OBS + h * 128
                buf[h, :, o : o + 128] = points[k][:, at : at + 128]
    part = lax.rem(slab, 2)
    keep_ref[...] = buf[part]
    send_ref[...] = buf[1 - part]


def pick(slab, order, owner, cells, lists, weight, ensemble, after):
    return pl.pallas_call(
        pick_kernel,
        out_shape=[jax.ShapeDtypeStruct((PADDED, PART), f32)] * 2,
        in_specs=smem(5) + whole(2) + [pl.BlockSpec(memory_space=pl.ANY)],
        out_specs=whole(2),
        scratch_shapes=[pltpu.VMEM((UNROLL, PADDED, BLOCKS * OBS), f32)] * POINTS
        + [pltpu.VMEM((2, PADDED, PART), f32)],
        compiler_params=params(60),
        cost_estimate=cost(8),
        name="pick",
    )(slab, order, owner, cells, lists, weight, ensemble, after)


def window_kernel(chip_ref, *refs):
    near, far, out_ref = refs[0:2], refs[2:4], refs[-1]
    total = chip_ref[...] + near[0][...] + near[1][...]
    out_ref[:, 0:FAR] = total[:, 0:FAR] + far[0][...] + far[1][...]
    out_ref[:, FAR:PART] = total[:, FAR:PART]


def window(chip, near, far, firsts):
    return pl.pallas_call(
        window_kernel,
        out_shape=jax.ShapeDtypeStruct((PADDED, PART), f32),
        in_specs=whole(5) + [pl.BlockSpec(memory_space=pl.ANY)] * len(firsts),
        out_specs=pl.BlockSpec(memory_space=pltpu.VMEM),
        compiler_params=params(4),
        cost_estimate=cost(1),
        name="window",
    )(chip, *near, *far, *firsts)


def reach_kernel(here_ref, order_ref, owner_ref, cells_ref, radius_ref, after_ref, *refs):
    del after_ref
    count_ref, index_ref, chosen_ref, centre_ref, inverse_ref, wide_ref, place = refs
    slot = lax.broadcasted_iota(jnp.int32, (OBS, OBS), 0)
    column = lax.broadcasted_iota(jnp.int32, (OBS, OBS), 1)
    before = jnp.where(slot < column, f32(1.0), f32(0.0)).astype(bf16)
    begin = (here_ref[0] * CELLS).astype(f32)
    end = begin + f32(CELLS - 1)
    place[:, 0:OBS] = jnp.zeros((1, OBS), f32)
    for t in range(BLOCKS):
        b = order_ref[t]
        everywhere = (owner_ref[pl.ds(b, 1), :] * CELLS + cells_ref[b]).astype(f32)
        if t > 0:
            for k in range(POINTS):
                o = OBS + (t - 1) * POINTS * OBS + k * OBS
                place[:, o : o + OBS] = everywhere[k : k + 1, :]
        centre = everywhere[0:1, :]
        radius = radius_ref[pl.ds(b, 1), :].astype(f32)
        inverse = f32(1.0) / radius
        terms = jnp.concatenate([centre, inverse, jnp.zeros((6, OBS), f32)], axis=0).T
        wide_ref[t, 0] = jnp.broadcast_to(terms[:, 0:1], (OBS, 128))
        wide_ref[t, 1] = jnp.broadcast_to(terms[:, 1:2], (OBS, 128))
        away = jnp.maximum(jnp.maximum(begin - centre, centre - end), f32(0.0))
        active = jnp.where(away < radius, f32(1.0), f32(0.0))
        count_ref[t] = jnp.sum(active).astype(jnp.int32)
        ahead = jnp.dot(jnp.broadcast_to(active, (8, OBS)).astype(bf16), before, preferred_element_type=f32)
        index = jnp.where(active > 0, ahead[0:1, :], f32(-1.0)).astype(jnp.int32)
        index_ref[t] = index
        hit = index == slot
        chosen_ref[t] = jnp.where(hit, f32(1.0), f32(0.0)).astype(bf16)
        centre_ref[t] = jnp.broadcast_to(jnp.sum(jnp.where(hit, centre, f32(0.0)), axis=1, keepdims=True), (OBS, 128))
        inverse_ref[t] = jnp.broadcast_to(jnp.sum(jnp.where(hit, inverse, f32(0.0)), axis=1, keepdims=True), (OBS, 128))


def reach(here, order, owner, cells, radius, first):
    shape = jax.ShapeDtypeStruct
    return pl.pallas_call(
        reach_kernel,
        out_shape=[
            shape((BLOCKS,), jnp.int32),
            shape((BLOCKS, 1, OBS), jnp.int32),
            shape((BLOCKS, OBS, OBS), bf16),
            shape((BLOCKS, OBS, 128), f32),
            shape((BLOCKS, OBS, 128), f32),
            shape((BLOCKS, 2, OBS, 128), f32),
            shape((1, COLS), f32),
        ],
        in_specs=smem(2) + whole(3) + [pl.BlockSpec(memory_space=pl.ANY)],
        out_specs=smem(1) + whole(6),
        compiler_params=params(60),
        cost_estimate=cost(2),
        name="reach",
    )(here, order, owner, cells, radius, first)


def updated(x, place, lhs, driver, centre, inverse, slots):
    reps = x.shape[1] // 128
    mean = jnp.sum(x, axis=0, keepdims=True) * f32(1.0 / MEMBERS)
    hi, lo = split(x - mean)
    cov = jnp.dot(lhs, jnp.concatenate([hi, lo, hi], axis=0), preferred_element_type=f32)
    centre = jnp.concatenate([centre] * reps, axis=1)
    inverse = jnp.concatenate([inverse] * reps, axis=1)
    loc = jnp.maximum(f32(0.0), f32(1.0) - jnp.abs(place - centre) * inverse)
    hi, lo = split(loc * cov)
    if slots == 64:
        return x + jnp.dot(driver, jnp.concatenate([hi, lo, hi], axis=0), preferred_element_type=f32)
    if slots == 128:
        both = jnp.dot(driver, jnp.concatenate([hi, lo], axis=0), preferred_element_type=f32)
        return x + (both[:MEMBERS] + both[MEMBERS:])
    both = jnp.dot(driver, hi, preferred_element_type=f32)
    rest = jnp.dot(driver[:MEMBERS], lo, preferred_element_type=f32)
    return x + (both[:MEMBERS] + both[MEMBERS:] + rest)


def drivers_kernel(here_ref, order_ref, count_ref, *refs):
    weight_ref, value_ref, variance_ref, index_ref, chosen_ref, wide, place, mine_ref, other_ref = refs[:9]
    lhs_ref, driver_ref, z, full, whole_lhs = refs[9:]
    part = lax.rem(here_ref[0] // GROUPS, 2)
    for src, h in ((mine_ref, part), (other_ref, 1 - part)):
        for p in range(GROUPS):
            for i in range(PART // 128):
                cols = slice(i * 128, i * 128 + 128)
                at = pl.ds(pl.multiple_of(i * OBS + h * 128, 128), 128)
                z[16 * p : 16 * p + 16, at] = src[PADDED * p : PADDED * p + 16, cols]
                z[64 + 4 * p : 68 + 4 * p, at] = src[PADDED * p + 16 : PADDED * p + 20, cols]

    for t in range(BLOCKS):
        b = order_ref[t]
        start = OBS + (t - 1) * POINTS * OBS
        weight = weight_ref[b]
        if t == 0:
            prior = z[:, 0:OBS]
        else:
            prior = z[:, start : start + OBS] * weight[0:1, :]
            for k in range(1, POINTS):
                prior = prior + z[:, start + k * OBS : start + (k + 1) * OBS] * weight[k : k + 1, :]
        value = value_ref[pl.ds(b, 1), :]
        variance = variance_ref[pl.ds(b, 1), :]
        ybar = jnp.sum(prior, axis=0, keepdims=True) * f32(1.0 / MEMBERS)
        anomaly = prior - ybar
        spread = jnp.sum(anomaly * anomaly, axis=0, keepdims=True) * f32(1.0 / (MEMBERS - 1))
        gain = f32(1.0) / (spread + variance)
        shrink = -gain / (f32(1.0) + jnp.sqrt(variance * gain))
        coeff = gain * (value - ybar)
        driver = coeff + shrink * anomaly
        hi, lo = split((anomaly * f32(1.0 / (MEMBERS - 1))).T)
        lhs = jnp.concatenate([hi, hi, lo], axis=1)
        dhi, dlo = split(driver)
        both = jnp.concatenate([dhi, dlo], axis=0)

        if t < BLOCKS - 1:
            whole_lhs[...] = lhs
            full[...] = both

            def evolve(i, carry):
                cols = pl.ds(pl.multiple_of(OBS + i * WIDE, 128), WIDE)
                z[:, cols] = updated(z[:, cols], place[:, cols], whole_lhs[...], full[...], wide[t, 0], wide[t, 1], OBS)
                return carry

            lax.fori_loop(t * POINTS * OBS // WIDE, (BLOCKS - 1) * POINTS * OBS // WIDE, evolve, 0)

        count = count_ref[t]
        lhs_ref[t] = jnp.dot(chosen_ref[t], lhs, preferred_element_type=f32).astype(bf16)
        nt = (((1,), (1,)), ((), ()))

        @pl.when(count <= 64)
        def _():
            slot = lax.broadcasted_iota(jnp.int32, (OBS, OBS), 0)
            again = jnp.where(index_ref[t] == (slot & 63), f32(1.0), f32(0.0)).astype(bf16)
            kept = lax.dot_general(both, again, nt, preferred_element_type=f32)
            lane = lax.broadcasted_iota(jnp.int32, (MEMBERS, OBS), 1)
            driver_ref[t, 0:MEMBERS] = jnp.where(lane < 128, kept[:MEMBERS], kept[MEMBERS:]).astype(bf16)

        @pl.when(count > 64)
        def _():
            kept = lax.dot_general(both, chosen_ref[t], nt, preferred_element_type=f32).astype(bf16)
            driver_ref[t] = kept

            @pl.when(count <= 128)
            def _():
                driver_ref[t, 0:MEMBERS, 128:256] = kept[:MEMBERS, 0:128]
                driver_ref[t, MEMBERS : 2 * MEMBERS, 128:256] = jnp.zeros((MEMBERS, 128), bf16)


def drivers(here, order, count, weight, value, variance, index, chosen, wide, place, mine, other):
    return pl.pallas_call(
        drivers_kernel,
        out_shape=[
            jax.ShapeDtypeStruct((BLOCKS, OBS, 3 * MEMBERS), bf16),
            jax.ShapeDtypeStruct((BLOCKS, 2 * MEMBERS, OBS), bf16),
        ],
        in_specs=smem(3) + whole(9),
        out_specs=whole(2),
        scratch_shapes=[
            pltpu.VMEM((MEMBERS, COLS), f32),
            pltpu.VMEM((2 * MEMBERS, OBS), bf16),
            pltpu.VMEM((OBS, 3 * MEMBERS), bf16),
        ],
        compiler_params=params(60),
        cost_estimate=cost(8),
        name="drivers",
    )(here, order, count, weight, value, variance, index, chosen, wide, place, mine, other)


def update_kernel(chunk, late, apart, here_ref, count_ref, lhs_ref, driver_ref, centre_ref, inverse_ref, *refs):
    n_in = GROUPS if late else 1
    given, made = refs[:n_in], refs[-3 - (GROUPS if apart else 1) :]
    x, in_ref, out_ref = made[-3:]
    if late:
        for d in range(GROUPS):
            in_ref[lax.rem(here_ref[0] + GROUPS - d, GROUPS)] = given[d][...]
    else:
        in_ref = given[0]
    if not apart:
        out_ref = made[0]
    ins = [in_ref.at[q] for q in range(GROUPS)]
    outs = [out_ref.at[q] for q in range(GROUPS)]
    low = lax.broadcasted_iota(jnp.int32, (8, HALF), 0) < 4
    offsets = lax.broadcasted_iota(jnp.int32, (1, HALF), 1)
    first = here_ref[0] * CELLS + (chunk + pl.program_id(0)) * CHUNK

    def join(a, b):
        return jnp.where(low, a, pltpu.roll(b, 4, 0)), jnp.where(low, pltpu.roll(a, 4, 0), b)

    for p, ref in enumerate(ins):
        for h in range(2):
            x[h, 16 * p : 16 * p + 8] = ref[:, h * HALF : (h + 1) * HALF]
            x[h, 16 * p + 8 : 16 * p + 16] = ref[:, CHUNK + h * HALF : CHUNK + (h + 1) * HALF]
    for q in range(2):
        rest = join(ins[2 * q][:, 2 * CHUNK : PACKED], ins[2 * q + 1][:, 2 * CHUNK : PACKED])
        for h in range(2):
            x[h, 64 + 8 * q : 72 + 8 * q] = rest[h]

    def block(t, carry):
        count = count_ref[t]

        def apply(slots):
            width = 192 if slots == 64 else OBS
            height = MEMBERS if slots == 64 else 2 * MEMBERS
            lhs = lhs_ref[t, 0:slots]
            driver = driver_ref[t, 0:height, 0:width]
            for h in range(2):
                place = (first + h * HALF + offsets).astype(f32)
                x[h] = updated(x[h], place, lhs, driver, centre_ref[t, 0:slots], inverse_ref[t, 0:slots], slots)

        @pl.when((count > 0) & (count <= 64))
        def _():
            apply(64)

        @pl.when((count > 64) & (count <= 128))
        def _():
            apply(128)

        @pl.when(count > 128)
        def _():
            apply(OBS)

        return carry

    lax.fori_loop(0, BLOCKS, block, 0)
    for p, ref in enumerate(outs):
        for h in range(2):
            ref[:, h * HALF : (h + 1) * HALF] = x[h, 16 * p : 16 * p + 8]
            ref[:, CHUNK + h * HALF : CHUNK + (h + 1) * HALF] = x[h, 16 * p + 8 : 16 * p + 16]
    for q in range(2):
        a, b = join(x[0, 64 + 8 * q : 72 + 8 * q], x[1, 64 + 8 * q : 72 + 8 * q])
        outs[2 * q][:, 2 * CHUNK : PACKED] = a
        outs[2 * q + 1][:, 2 * CHUNK : PACKED] = b
    if apart:
        for d in range(GROUPS):
            made[d][...] = out_ref[lax.rem(here_ref[0] + d, GROUPS)]


def fixed(shape, index):
    return pl.BlockSpec(shape, lambda i: index, pipeline_mode=pl.Buffered(1))


def update(chunks, late, apart, index, here, terms, arrived, firsts):
    gathered = (GROUPS, 8, PACKED)
    shapes = [gathered[1:]] * GROUPS if apart else [gathered]
    n = len(chunks)

    def wide(shape):
        return jax.ShapeDtypeStruct(shape[:-1] + (PACKED * n,), f32)

    def blocks(shape, at):
        return pl.BlockSpec(shape, lambda i: (0,) * (len(shape) - 1) + (at + i,))

    return pl.pallas_call(
        functools.partial(update_kernel, chunks[0], late, apart),
        grid=(n,),
        out_shape=[wide(shape) for shape in shapes],
        in_specs=smem(2)
        + [fixed(a.shape, (0, 0, 0)) for a in terms[1:]]
        + ([blocks(gathered[1:], index)] * GROUPS if late else [blocks(gathered, index)])
        + [pl.BlockSpec(memory_space=pl.ANY)] * len(firsts),
        out_specs=[blocks(shape, 0) for shape in shapes],
        scratch_shapes=[pltpu.VMEM((2, MEMBERS, HALF), f32)] + [pltpu.VMEM(gathered, f32)] * 2,
        compiler_params=params(60),
        cost_estimate=cost(8),
        name="update",
    )(here, *terms, *arrived, *firsts)


def unpack_kernel(chunk, apart, rank_ref, *refs):
    out_ref, rows, sems = refs[-3:]
    copies = []
    for i in range(GROUPS):
        src = refs[i] if apart else refs[0].at[i]
        quarter = lax.rem(rank_ref[0] + GROUPS - i, GROUPS) if apart else i
        rows[i, 0:8, :] = src[:, 0:CHUNK]
        rows[i, 8:16, :] = src[:, CHUNK : 2 * CHUNK]
        rows[i, 16:20, 0:HALF] = src[0:4, 2 * CHUNK : PACKED]
        rows[i, 16:20, HALF:CHUNK] = src[4:8, 2 * CHUNK : PACKED]
        at = pl.multiple_of(quarter * CELLS + (chunk + pl.program_id(0)) * CHUNK, 128)
        copy = pltpu.make_async_copy(rows.at[i], out_ref.at[:, pl.ds(at, CHUNK)], sems.at[i])
        copy.start()
        copies.append(copy)
    for copy in copies:
        copy.wait()


def unpack(chunks, apart, rank, pieces, out):
    held = [] if out is None else [out]
    shape = (8, PACKED) if apart else (GROUPS, 8, PACKED)
    block = pl.BlockSpec(shape, lambda i: (0,) * (len(shape) - 1) + (i,))
    return pl.pallas_call(
        functools.partial(unpack_kernel, chunks[0], apart),
        grid=(len(chunks),),
        out_shape=jax.ShapeDtypeStruct((ROWS, GROUPS * CELLS), f32),
        in_specs=smem(1) + [block] * len(pieces) + [pl.BlockSpec(memory_space=pl.ANY)] * len(held),
        out_specs=pl.BlockSpec(memory_space=pl.ANY),
        scratch_shapes=[pltpu.VMEM((GROUPS, ROWS, CHUNK), f32), pltpu.SemaphoreType.DMA((GROUPS,))],
        input_output_aliases={1 + len(pieces): 0} if held else {},
        compiler_params=params(8),
        cost_estimate=cost(2),
        name="unpack",
    )(rank, *pieces, *held)


def shifted(x, axis, size, by):
    return lax.ppermute(x, axis, [(i, (i + by) % size) for i in range(size)])


def exchanged(x):
    return lax.all_to_all(x, "member", split_axis=0, concat_axis=0, tiled=True)


def per_device(
    ensemble,
    block_order,
    obs_owner,
    interp_cells,
    interp_weight,
    obs_radius,
    obs_value,
    obs_variance,
):
    slabs = lax.axis_size("slab")
    member_rank = lax.axis_index("member")
    slab_rank = lax.axis_index("slab")
    rank = member_rank.reshape(1)
    slab = slab_rank.reshape(1)
    here = slab * GROUPS + rank

    cells = interp_cells.transpose(0, 2, 1)
    weight = interp_weight.transpose(0, 2, 1)
    early, *late, lists = pack(rank, slab, block_order, obs_owner, ensemble)
    entered = [exchanged(early)]
    keep, send = pick(slab, block_order, obs_owner, cells, lists, weight, ensemble, early)
    chip = keep + lax.ppermute(send, "slab", [(i, i ^ 1) for i in range(slabs)])
    near = [shifted(chip, "slab", slabs, by) for by in (2, -2)]
    far = [shifted(chip[:, :FAR], "slab", slabs, by) for by in (4, -4)]
    count, index, chosen, centre, inverse, wide, place = reach(
        here, block_order, obs_owner, cells, obs_radius, chip
    )
    summed = window(chip, near, far, [count])
    mine = lax.all_gather(summed, "member", axis=0, tiled=True)
    other = lax.ppermute(mine, "slab", [(i, i ^ 1) for i in range(slabs)])
    late = after(late, mine, entered[0][0, :, 0:128])
    late = [late[0]] + [shifted(late[d], "member", GROUPS, d) for d in range(1, GROUPS)]
    lhs, driver = drivers(
        here, block_order, count, weight, obs_value, obs_variance, index, chosen, wide, place, mine, other
    )
    terms = (count, lhs, driver, centre, inverse)

    made, firsts = [], []
    for e, chunks in enumerate(EXITS):
        held = chunks[0] in LATE
        group = LATE if held else EARLY
        at = group.index(chunks[0])
        new = update(chunks, held, e > 0, at, here, terms, late if held else entered, firsts)
        if e == 0:
            new = after(new, *late[1:])
        made.append(new)
        firsts = [new[0]]
    out = None
    for e, (chunks, new) in enumerate(zip(EXITS, made)):
        if e == 0:
            back = [exchanged(new[0])]
        else:
            back = [new[0]] + [shifted(new[d], "member", GROUPS, d) for d in range(1, GROUPS)]
        out = unpack(chunks, e > 0, rank, back, out)
    return out


def solution(mesh):
    in_specs = (P("member", "slab"), P(), P(), P(), P(), P(), P(), P())
    out_specs = P("member", "slab")
    return jax.shard_map(
        per_device, mesh=mesh, in_specs=in_specs, out_specs=out_specs, check_vma=False
    )
```

```python
import functools

import jax
import jax.numpy as jnp
from jax import lax
from jax.experimental import pallas as pl
from jax.experimental.pallas import tpu as pltpu
from jax.sharding import PartitionSpec as P

MEMBERS = 80
BLOCKS = 4
POINTS = 4
OBS = 256
GROUPS = 4
ROWS = MEMBERS // GROUPS
PADDED = 24
CELLS = 12288
CHUNKS = 6
EARLY = (0, 1, 2, 3)
LATE = (4, 5)
EXITS = ((0, 1), (2, 3), (4, 5))
CHUNK = CELLS // CHUNKS
HALF = CHUNK // 2
PACKED = 5 * HALF
COLS = OBS + (BLOCKS - 1) * POINTS * OBS
PART = COLS // 2
FAR = 128 + POINTS * 128
WIDE = 1024
UNROLL = 8
MIB = 1024 * 1024

f32 = jnp.float32
bf16 = jnp.bfloat16


def split(x):
    hi = x.astype(bf16)
    lo = (x - hi.astype(f32)).astype(bf16)
    return hi, lo


def whole(n):
    return [pl.BlockSpec(memory_space=pltpu.VMEM)] * n


def smem(n):
    return [pl.BlockSpec(memory_space=pltpu.SMEM)] * n


def params(mib):
    return pltpu.CompilerParams(vmem_limit_bytes=mib * MIB)


def cost(micros):
    return pl.CostEstimate(flops=0, bytes_accessed=int(micros * 1024), transcendentals=0)


def place_piece(out, o, ens_ref, c):
    at, mid = c * CHUNK, c * CHUNK + HALF
    out[:, o : o + CHUNK] = ens_ref[0:8, at : at + CHUNK]
    out[:, o + CHUNK : o + 2 * CHUNK] = ens_ref[8:16, at : at + CHUNK]
    out[0:4, o + 2 * CHUNK : o + PACKED] = ens_ref[16:20, at : at + HALF]
    out[4:8, o + 2 * CHUNK : o + PACKED] = ens_ref[16:20, mid : mid + HALF]


def pack_kernel(rank_ref, slab_ref, order_ref, owner_ref, ens_ref, early_ref, *refs):
    late_refs, lists_ref, owners = refs[:GROUPS], refs[GROUPS], refs[GROUPS + 1]
    step = pl.program_id(0)

    @pl.when(step == 1)
    def _():
        owners[...] = jnp.full_like(owners, -1)
        for t in range(BLOCKS):
            owners[t : t + 1, :] = owner_ref[pl.ds(order_ref[t], 1), :]
        row = lax.broadcasted_iota(jnp.int32, (OBS, OBS), 0)
        column = lax.broadcasted_iota(jnp.int32, (OBS, OBS), 1)
        before = jnp.where(row < column, f32(1.0), f32(0.0)).astype(bf16)
        inside = (owners[...] >> 2) == slab_ref[0]
        ahead = jnp.dot(jnp.where(inside, f32(1.0), f32(0.0)).astype(bf16), before, preferred_element_type=f32)
        index = jnp.where(inside, ahead, f32(-1.0)).T
        for t in range(BLOCKS):
            hit = index[:, t : t + 1] == column.astype(f32)
            held = jnp.sum(jnp.where(hit, row.astype(f32), f32(0.0)), axis=0, keepdims=True)
            lists_ref[t : t + 1, :] = held.astype(jnp.int32)
        total = jnp.sum(jnp.where(inside, f32(1.0), f32(0.0)), axis=1, keepdims=True)
        lists_ref[BLOCKS : 2 * BLOCKS, :] = jnp.broadcast_to(total[0:BLOCKS], (BLOCKS, OBS)).astype(jnp.int32)

    for i, c in enumerate(EARLY):
        place_piece(early_ref.at[0], i * PACKED, ens_ref, c)
    for d in range(GROUPS):

        @pl.when(step == d)
        def _():
            for i, c in enumerate(LATE):
                place_piece(late_refs[d], i * PACKED, ens_ref, c)


def pack(rank, slab, order, owner, ensemble):
    late = jax.ShapeDtypeStruct((8, PACKED * len(LATE)), f32)

    def quarter(i, rank_ref):
        return lax.rem(rank_ref[0] + i, GROUPS)

    return pl.pallas_call(
        pack_kernel,
        grid_spec=pltpu.PrefetchScalarGridSpec(
            num_scalar_prefetch=3,
            grid=(GROUPS,),
            in_specs=[
                pl.BlockSpec((BLOCKS, OBS), lambda i, *_: (0, 0)),
                pl.BlockSpec((ROWS, CELLS), lambda i, r, *_: (0, quarter(i, r))),
            ],
            out_specs=[pl.BlockSpec((1, 8, PACKED * len(EARLY)), lambda i, r, *_: (quarter(i, r), 0, 0))]
            + [pl.BlockSpec(late.shape, lambda i, *_: (0, 0))] * GROUPS
            + [pl.BlockSpec((2 * BLOCKS, OBS), lambda i, *_: (0, 0))],
            scratch_shapes=[pltpu.VMEM((2 * BLOCKS, OBS), jnp.int32)],
        ),
        out_shape=[jax.ShapeDtypeStruct((GROUPS, 8, PACKED * len(EARLY)), f32)]
        + [late] * GROUPS
        + [jax.ShapeDtypeStruct((2 * BLOCKS, OBS), jnp.int32)],
        compiler_params=params(60),
        cost_estimate=cost(3),
        name="pack",
    )(rank, slab, order, owner, ensemble)


def after_kernel(*refs):
    pass


def after(xs, *firsts):
    anywhere = pl.BlockSpec(memory_space=pl.ANY)
    n = len(xs)
    return pl.pallas_call(
        after_kernel,
        out_shape=[jax.ShapeDtypeStruct(x.shape, x.dtype) for x in xs],
        in_specs=[anywhere] * (n + len(firsts)),
        out_specs=[anywhere] * n,
        input_output_aliases={i: i for i in range(n)},
        compiler_params=params(60),
        cost_estimate=cost(1),
        name="after",
    )(*xs, *firsts)


def pick_kernel(slab_ref, order_ref, owner_ref, cells_ref, held, weight_ref, ens_ref, after_ref, keep_ref, send_ref, *bufs):
    del after_ref
    slab = slab_ref[0]
    buf = bufs[POINTS]
    for point in bufs[:POINTS]:
        point[...] = jnp.zeros_like(point)

    blocks = [order_ref[t] for t in range(BLOCKS)]
    lanes = lax.broadcasted_iota(jnp.int32, (8, 128), 1)
    lanes4 = lax.broadcasted_iota(jnp.int32, (4, 128), 1)
    for t in range(BLOCKS):
        count = held[BLOCKS + t, 0]
        b = blocks[t]

        def some(s, carry):
            for u in range(UNROLL):
                i = s * UNROLL + u
                valid = i < count
                j = jnp.where(valid, held[t, i], 0)
                base = (owner_ref[b, j] & 3) * CELLS
                n = j & 127
                lane = jnp.where(valid, n, -1)
                hit = lanes == lane
                hit4 = lanes4 == lane
                dst = pl.ds(pl.multiple_of(t * OBS + (j - n), 128), 128)
                for k in range(POINTS):
                    point = bufs[k].at[u]
                    place = jnp.where(valid, base + cells_ref[b, k, j], 0)
                    src = pl.ds(pl.multiple_of((place >> 7) * 128, 128), 128)
                    shift = (n - place) & 127
                    point[0:8, dst] = jnp.where(hit, pltpu.roll(ens_ref[0:8, src], shift, 1), point[0:8, dst])
                    point[8:16, dst] = jnp.where(hit, pltpu.roll(ens_ref[8:16, src], shift, 1), point[8:16, dst])
                    point[16:20, dst] = jnp.where(hit4, pltpu.roll(ens_ref[16:20, src], shift, 1), point[16:20, dst])
            return carry

        lax.fori_loop(0, (count + UNROLL - 1) // UNROLL, some, 0)
    points = [sum(point[u] for u in range(1, UNROLL)) + point[0] for point in bufs[:POINTS]]
    weight = weight_ref[blocks[0]]
    total = points[0][:, 0:OBS] * weight[0:1, :]
    for k in range(1, POINTS):
        total = total + points[k][:, 0:OBS] * weight[k : k + 1, :]
    for h in range(2):
        half = slice(h * 128, h * 128 + 128)
        buf[h, :, 0:128] = total[:, half]
        for t in range(1, BLOCKS):
            for k in range(POINTS):
                o = 128 + ((t - 1) * POINTS + k) * 128
                at = t * OBS + h * 128
                buf[h, :, o : o + 128] = points[k][:, at : at + 128]
    part = lax.rem(slab, 2)
    keep_ref[...] = buf[part]
    send_ref[...] = buf[1 - part]


def pick(slab, order, owner, cells, lists, weight, ensemble, after):
    return pl.pallas_call(
        pick_kernel,
        out_shape=[jax.ShapeDtypeStruct((PADDED, PART), f32)] * 2,
        in_specs=smem(5) + whole(2) + [pl.BlockSpec(memory_space=pl.ANY)],
        out_specs=whole(2),
        scratch_shapes=[pltpu.VMEM((UNROLL, PADDED, BLOCKS * OBS), f32)] * POINTS
        + [pltpu.VMEM((2, PADDED, PART), f32)],
        compiler_params=params(60),
        cost_estimate=cost(8),
        name="pick",
    )(slab, order, owner, cells, lists, weight, ensemble, after)


def window_kernel(chip_ref, *refs):
    near, far, out_ref = refs[0:2], refs[2:4], refs[-1]
    total = chip_ref[...] + near[0][...] + near[1][...]
    out_ref[:, 0:FAR] = total[:, 0:FAR] + far[0][...] + far[1][...]
    out_ref[:, FAR:PART] = total[:, FAR:PART]


def window(chip, near, far, firsts):
    return pl.pallas_call(
        window_kernel,
        out_shape=jax.ShapeDtypeStruct((PADDED, PART), f32),
        in_specs=whole(5) + [pl.BlockSpec(memory_space=pl.ANY)] * len(firsts),
        out_specs=pl.BlockSpec(memory_space=pltpu.VMEM),
        compiler_params=params(4),
        cost_estimate=cost(1),
        name="window",
    )(chip, *near, *far, *firsts)


def reach_kernel(here_ref, order_ref, owner_ref, cells_ref, radius_ref, after_ref, *refs):
    del after_ref
    count_ref, index_ref, chosen_ref, centre_ref, inverse_ref, wide_ref, place = refs
    slot = lax.broadcasted_iota(jnp.int32, (OBS, OBS), 0)
    column = lax.broadcasted_iota(jnp.int32, (OBS, OBS), 1)
    before = jnp.where(slot < column, f32(1.0), f32(0.0)).astype(bf16)
    begin = (here_ref[0] * CELLS).astype(f32)
    end = begin + f32(CELLS - 1)
    place[:, 0:OBS] = jnp.zeros((1, OBS), f32)
    for t in range(BLOCKS):
        b = order_ref[t]
        everywhere = (owner_ref[pl.ds(b, 1), :] * CELLS + cells_ref[b]).astype(f32)
        if t > 0:
            for k in range(POINTS):
                o = OBS + (t - 1) * POINTS * OBS + k * OBS
                place[:, o : o + OBS] = everywhere[k : k + 1, :]
        centre = everywhere[0:1, :]
        radius = radius_ref[pl.ds(b, 1), :].astype(f32)
        inverse = f32(1.0) / radius
        terms = jnp.concatenate([centre, inverse, jnp.zeros((6, OBS), f32)], axis=0).T
        wide_ref[t, 0] = jnp.broadcast_to(terms[:, 0:1], (OBS, 128))
        wide_ref[t, 1] = jnp.broadcast_to(terms[:, 1:2], (OBS, 128))
        away = jnp.maximum(jnp.maximum(begin - centre, centre - end), f32(0.0))
        active = jnp.where(away < radius, f32(1.0), f32(0.0))
        count_ref[t] = jnp.sum(active).astype(jnp.int32)
        ahead = jnp.dot(jnp.broadcast_to(active, (8, OBS)).astype(bf16), before, preferred_element_type=f32)
        index = jnp.where(active > 0, ahead[0:1, :], f32(-1.0)).astype(jnp.int32)
        index_ref[t] = index
        hit = index == slot
        chosen_ref[t] = jnp.where(hit, f32(1.0), f32(0.0)).astype(bf16)
        centre_ref[t] = jnp.broadcast_to(jnp.sum(jnp.where(hit, centre, f32(0.0)), axis=1, keepdims=True), (OBS, 128))
        inverse_ref[t] = jnp.broadcast_to(jnp.sum(jnp.where(hit, inverse, f32(0.0)), axis=1, keepdims=True), (OBS, 128))


def reach(here, order, owner, cells, radius, first):
    shape = jax.ShapeDtypeStruct
    return pl.pallas_call(
        reach_kernel,
        out_shape=[
            shape((BLOCKS,), jnp.int32),
            shape((BLOCKS, 1, OBS), jnp.int32),
            shape((BLOCKS, OBS, OBS), bf16),
            shape((BLOCKS, OBS, 128), f32),
            shape((BLOCKS, OBS, 128), f32),
            shape((BLOCKS, 2, OBS, 128), f32),
            shape((1, COLS), f32),
        ],
        in_specs=smem(2) + whole(3) + [pl.BlockSpec(memory_space=pl.ANY)],
        out_specs=smem(1) + whole(6),
        compiler_params=params(60),
        cost_estimate=cost(2),
        name="reach",
    )(here, order, owner, cells, radius, first)


def updated(x, place, lhs, driver, centre, inverse, slots):
    reps = x.shape[1] // 128
    mean = jnp.sum(x, axis=0, keepdims=True) * f32(1.0 / MEMBERS)
    hi, lo = split(x - mean)
    cov = jnp.dot(lhs, jnp.concatenate([hi, lo, hi], axis=0), preferred_element_type=f32)
    centre = jnp.concatenate([centre] * reps, axis=1)
    inverse = jnp.concatenate([inverse] * reps, axis=1)
    loc = jnp.maximum(f32(0.0), f32(1.0) - jnp.abs(place - centre) * inverse)
    hi, lo = split(loc * cov)
    if slots == 64:
        return x + jnp.dot(driver, jnp.concatenate([hi, lo, hi], axis=0), preferred_element_type=f32)
    if slots == 128:
        both = jnp.dot(driver, jnp.concatenate([hi, lo], axis=0), preferred_element_type=f32)
        return x + (both[:MEMBERS] + both[MEMBERS:])
    both = jnp.dot(driver, hi, preferred_element_type=f32)
    rest = jnp.dot(driver[:MEMBERS], lo, preferred_element_type=f32)
    return x + (both[:MEMBERS] + both[MEMBERS:] + rest)


def drivers_kernel(here_ref, order_ref, count_ref, *refs):
    weight_ref, value_ref, variance_ref, index_ref, chosen_ref, wide, place, mine_ref, other_ref = refs[:9]
    lhs_ref, driver_ref, z, full, whole_lhs = refs[9:]
    part = lax.rem(here_ref[0] // GROUPS, 2)
    for src, h in ((mine_ref, part), (other_ref, 1 - part)):
        for p in range(GROUPS):
            for i in range(PART // 128):
                cols = slice(i * 128, i * 128 + 128)
                at = pl.ds(pl.multiple_of(i * OBS + h * 128, 128), 128)
                z[16 * p : 16 * p + 16, at] = src[PADDED * p : PADDED * p + 16, cols]
                z[64 + 4 * p : 68 + 4 * p, at] = src[PADDED * p + 16 : PADDED * p + 20, cols]

    for t in range(BLOCKS):
        b = order_ref[t]
        start = OBS + (t - 1) * POINTS * OBS
        weight = weight_ref[b]
        if t == 0:
            prior = z[:, 0:OBS]
        else:
            prior = z[:, start : start + OBS] * weight[0:1, :]
            for k in range(1, POINTS):
                prior = prior + z[:, start + k * OBS : start + (k + 1) * OBS] * weight[k : k + 1, :]
        value = value_ref[pl.ds(b, 1), :]
        variance = variance_ref[pl.ds(b, 1), :]
        ybar = jnp.sum(prior, axis=0, keepdims=True) * f32(1.0 / MEMBERS)
        anomaly = prior - ybar
        spread = jnp.sum(anomaly * anomaly, axis=0, keepdims=True) * f32(1.0 / (MEMBERS - 1))
        gain = f32(1.0) / (spread + variance)
        shrink = -gain / (f32(1.0) + jnp.sqrt(variance * gain))
        coeff = gain * (value - ybar)
        driver = coeff + shrink * anomaly
        hi, lo = split((anomaly * f32(1.0 / (MEMBERS - 1))).T)
        lhs = jnp.concatenate([hi, hi, lo], axis=1)
        dhi, dlo = split(driver)
        both = jnp.concatenate([dhi, dlo], axis=0)

        if t < BLOCKS - 1:
            whole_lhs[...] = lhs
            full[...] = both

            def evolve(i, carry):
                cols = pl.ds(pl.multiple_of(OBS + i * WIDE, 128), WIDE)
                z[:, cols] = updated(z[:, cols], place[:, cols], whole_lhs[...], full[...], wide[t, 0], wide[t, 1], OBS)
                return carry

            lax.fori_loop(t * POINTS * OBS // WIDE, (BLOCKS - 1) * POINTS * OBS // WIDE, evolve, 0)

        count = count_ref[t]
        lhs_ref[t] = jnp.dot(chosen_ref[t], lhs, preferred_element_type=f32).astype(bf16)
        nt = (((1,), (1,)), ((), ()))

        @pl.when(count <= 64)
        def _():
            slot = lax.broadcasted_iota(jnp.int32, (OBS, OBS), 0)
            again = jnp.where(index_ref[t] == (slot & 63), f32(1.0), f32(0.0)).astype(bf16)
            kept = lax.dot_general(both, again, nt, preferred_element_type=f32)
            lane = lax.broadcasted_iota(jnp.int32, (MEMBERS, OBS), 1)
            driver_ref[t, 0:MEMBERS] = jnp.where(lane < 128, kept[:MEMBERS], kept[MEMBERS:]).astype(bf16)

        @pl.when(count > 64)
        def _():
            kept = lax.dot_general(both, chosen_ref[t], nt, preferred_element_type=f32).astype(bf16)
            driver_ref[t] = kept

            @pl.when(count <= 128)
            def _():
                driver_ref[t, 0:MEMBERS, 128:256] = kept[:MEMBERS, 0:128]
                driver_ref[t, MEMBERS : 2 * MEMBERS, 128:256] = jnp.zeros((MEMBERS, 128), bf16)


def drivers(here, order, count, weight, value, variance, index, chosen, wide, place, mine, other):
    return pl.pallas_call(
        drivers_kernel,
        out_shape=[
            jax.ShapeDtypeStruct((BLOCKS, OBS, 3 * MEMBERS), bf16),
            jax.ShapeDtypeStruct((BLOCKS, 2 * MEMBERS, OBS), bf16),
        ],
        in_specs=smem(3) + whole(9),
        out_specs=whole(2),
        scratch_shapes=[
            pltpu.VMEM((MEMBERS, COLS), f32),
            pltpu.VMEM((2 * MEMBERS, OBS), bf16),
            pltpu.VMEM((OBS, 3 * MEMBERS), bf16),
        ],
        compiler_params=params(60),
        cost_estimate=cost(8),
        name="drivers",
    )(here, order, count, weight, value, variance, index, chosen, wide, place, mine, other)


def update_kernel(chunk, late, apart, here_ref, count_ref, lhs_ref, driver_ref, centre_ref, inverse_ref, *refs):
    n_in = GROUPS if late else 1
    given, made = refs[:n_in], refs[-3 - (GROUPS if apart else 1) :]
    x, in_ref, out_ref = made[-3:]
    if late:
        for d in range(GROUPS):
            in_ref[lax.rem(here_ref[0] + GROUPS - d, GROUPS)] = given[d][...]
    else:
        in_ref = given[0]
    if not apart:
        out_ref = made[0]
    ins = [in_ref.at[q] for q in range(GROUPS)]
    outs = [out_ref.at[q] for q in range(GROUPS)]
    low = lax.broadcasted_iota(jnp.int32, (8, HALF), 0) < 4
    offsets = lax.broadcasted_iota(jnp.int32, (1, HALF), 1)
    first = here_ref[0] * CELLS + (chunk + pl.program_id(0)) * CHUNK

    def join(a, b):
        return jnp.where(low, a, pltpu.roll(b, 4, 0)), jnp.where(low, pltpu.roll(a, 4, 0), b)

    for p, ref in enumerate(ins):
        for h in range(2):
            x[h, 16 * p : 16 * p + 8] = ref[:, h * HALF : (h + 1) * HALF]
            x[h, 16 * p + 8 : 16 * p + 16] = ref[:, CHUNK + h * HALF : CHUNK + (h + 1) * HALF]
    for q in range(2):
        rest = join(ins[2 * q][:, 2 * CHUNK : PACKED], ins[2 * q + 1][:, 2 * CHUNK : PACKED])
        for h in range(2):
            x[h, 64 + 8 * q : 72 + 8 * q] = rest[h]

    def block(t, carry):
        count = count_ref[t]

        def apply(slots):
            width = 192 if slots == 64 else OBS
            height = MEMBERS if slots == 64 else 2 * MEMBERS
            lhs = lhs_ref[t, 0:slots]
            driver = driver_ref[t, 0:height, 0:width]
            for h in range(2):
                place = (first + h * HALF + offsets).astype(f32)
                x[h] = updated(x[h], place, lhs, driver, centre_ref[t, 0:slots], inverse_ref[t, 0:slots], slots)

        @pl.when((count > 0) & (count <= 64))
        def _():
            apply(64)

        @pl.when((count > 64) & (count <= 128))
        def _():
            apply(128)

        @pl.when(count > 128)
        def _():
            apply(OBS)

        return carry

    lax.fori_loop(0, BLOCKS, block, 0)
    for p, ref in enumerate(outs):
        for h in range(2):
            ref[:, h * HALF : (h + 1) * HALF] = x[h, 16 * p : 16 * p + 8]
            ref[:, CHUNK + h * HALF : CHUNK + (h + 1) * HALF] = x[h, 16 * p + 8 : 16 * p + 16]
    for q in range(2):
        a, b = join(x[0, 64 + 8 * q : 72 + 8 * q], x[1, 64 + 8 * q : 72 + 8 * q])
        outs[2 * q][:, 2 * CHUNK : PACKED] = a
        outs[2 * q + 1][:, 2 * CHUNK : PACKED] = b
    if apart:
        for d in range(GROUPS):
            made[d][...] = out_ref[lax.rem(here_ref[0] + d, GROUPS)]


def fixed(shape, index):
    return pl.BlockSpec(shape, lambda i: index, pipeline_mode=pl.Buffered(1))


def update(chunks, late, apart, index, here, terms, arrived, firsts):
    gathered = (GROUPS, 8, PACKED)
    shapes = [gathered[1:]] * GROUPS if apart else [gathered]
    n = len(chunks)

    def wide(shape):
        return jax.ShapeDtypeStruct(shape[:-1] + (PACKED * n,), f32)

    def blocks(shape, at):
        return pl.BlockSpec(shape, lambda i: (0,) * (len(shape) - 1) + (at + i,))

    return pl.pallas_call(
        functools.partial(update_kernel, chunks[0], late, apart),
        grid=(n,),
        out_shape=[wide(shape) for shape in shapes],
        in_specs=smem(2)
        + [fixed(a.shape, (0, 0, 0)) for a in terms[1:]]
        + ([blocks(gathered[1:], index)] * GROUPS if late else [blocks(gathered, index)])
        + [pl.BlockSpec(memory_space=pl.ANY)] * len(firsts),
        out_specs=[blocks(shape, 0) for shape in shapes],
        scratch_shapes=[pltpu.VMEM((2, MEMBERS, HALF), f32)] + [pltpu.VMEM(gathered, f32)] * 2,
        compiler_params=params(60),
        cost_estimate=cost(8),
        name="update",
    )(here, *terms, *arrived, *firsts)


def unpack_kernel(chunk, apart, rank_ref, *refs):
    out_ref, rows, sems = refs[-3:]
    copies = []
    for i in range(GROUPS):
        src = refs[i] if apart else refs[0].at[i]
        quarter = lax.rem(rank_ref[0] + GROUPS - i, GROUPS) if apart else i
        rows[i, 0:8, :] = src[:, 0:CHUNK]
        rows[i, 8:16, :] = src[:, CHUNK : 2 * CHUNK]
        rows[i, 16:20, 0:HALF] = src[0:4, 2 * CHUNK : PACKED]
        rows[i, 16:20, HALF:CHUNK] = src[4:8, 2 * CHUNK : PACKED]
        at = pl.multiple_of(quarter * CELLS + (chunk + pl.program_id(0)) * CHUNK, 128)
        copy = pltpu.make_async_copy(rows.at[i], out_ref.at[:, pl.ds(at, CHUNK)], sems.at[i])
        copy.start()
        copies.append(copy)
    for copy in copies:
        copy.wait()


def unpack(chunks, apart, rank, pieces, out):
    held = [] if out is None else [out]
    shape = (8, PACKED) if apart else (GROUPS, 8, PACKED)
    block = pl.BlockSpec(shape, lambda i: (0,) * (len(shape) - 1) + (i,))
    return pl.pallas_call(
        functools.partial(unpack_kernel, chunks[0], apart),
        grid=(len(chunks),),
        out_shape=jax.ShapeDtypeStruct((ROWS, GROUPS * CELLS), f32),
        in_specs=smem(1) + [block] * len(pieces) + [pl.BlockSpec(memory_space=pl.ANY)] * len(held),
        out_specs=pl.BlockSpec(memory_space=pl.ANY),
        scratch_shapes=[pltpu.VMEM((GROUPS, ROWS, CHUNK), f32), pltpu.SemaphoreType.DMA((GROUPS,))],
        input_output_aliases={1 + len(pieces): 0} if held else {},
        compiler_params=params(8),
        cost_estimate=cost(2),
        name="unpack",
    )(rank, *pieces, *held)


def shifted(x, axis, size, by):
    return lax.ppermute(x, axis, [(i, (i + by) % size) for i in range(size)])


def exchanged(x):
    return lax.all_to_all(x, "member", split_axis=0, concat_axis=0, tiled=True)


def per_device(
    ensemble,
    block_order,
    obs_owner,
    interp_cells,
    interp_weight,
    obs_radius,
    obs_value,
    obs_variance,
):
    slabs = lax.axis_size("slab")
    member_rank = lax.axis_index("member")
    slab_rank = lax.axis_index("slab")
    rank = member_rank.reshape(1)
    slab = slab_rank.reshape(1)
    here = slab * GROUPS + rank

    cells = interp_cells.transpose(0, 2, 1)
    weight = interp_weight.transpose(0, 2, 1)
    early, *late, lists = pack(rank, slab, block_order, obs_owner, ensemble)
    entered = [exchanged(early)]
    keep, send = pick(slab, block_order, obs_owner, cells, lists, weight, ensemble, early)
    chip = keep + lax.ppermute(send, "slab", [(i, i ^ 1) for i in range(slabs)])
    near = [shifted(chip, "slab", slabs, by) for by in (2, -2)]
    far = [shifted(chip[:, :FAR], "slab", slabs, by) for by in (4, -4)]
    count, index, chosen, centre, inverse, wide, place = reach(
        here, block_order, obs_owner, cells, obs_radius, chip
    )
    summed = window(chip, near, far, [count])
    mine = lax.all_gather(summed, "member", axis=0, tiled=True)
    other = lax.ppermute(mine, "slab", [(i, i ^ 1) for i in range(slabs)])
    late = after(late, mine, entered[0][0, :, 0:128])
    late = [late[0]] + [shifted(late[d], "member", GROUPS, d) for d in range(1, GROUPS)]
    lhs, driver = drivers(
        here, block_order, count, weight, obs_value, obs_variance, index, chosen, wide, place, mine, other
    )
    terms = (count, lhs, driver, centre, inverse)

    made, firsts = [], []
    for e, chunks in enumerate(EXITS):
        held = chunks[0] in LATE
        group = LATE if held else EARLY
        at = group.index(chunks[0])
        new = update(chunks, held, e > 0, at, here, terms, late if held else entered, firsts)
        if e == 0:
            new = after(new, *late[1:])
        made.append(new)
        firsts = [new[0]]
    out = None
    for e, (chunks, new) in enumerate(zip(EXITS, made)):
        if e == 0:
            back = [exchanged(new[0])]
        else:
            back = [new[0]] + [shifted(new[d], "member", GROUPS, d) for d in range(1, GROUPS)]
        out = unpack(chunks, e > 0, rank, back, out)
    return out


def solution(mesh):
    in_specs = (P("member", "slab"), P(), P(), P(), P(), P(), P(), P())
    out_specs = P("member", "slab")
    return jax.shard_map(
        per_device, mesh=mesh, in_specs=in_specs, out_specs=out_specs, check_vma=False
    )
```
